256 devices in a mesh: row: 64 (over x, z, core), col: 4 (over y).
Axes of the slice: x: 4, y: 4, z: 8, core: 2. Of those that a mesh axis runs over, the one named last changes fastest.
Arguments:
- matrix: float32 [65536, 4096], P('row', 'col'), may hold values from -80 to 80, as said below
Outputs:
- q_panels: float32 [65536, 512], P('row')
- coeff_rows: float32 [512, 4096], P(None, 'col')
- remainder: float32 [65536, 4096], P('row', 'col')
The draws below stay inside these ranges and needn't reach their ends.
Inputs may be any that keep to these rules, and one draw needn't show every extreme that they name: `matrix`: the first 512 columns have full column rank; the other columns are well conditioned against them.
All inputs are finite; a program needn't handle non-finite values.
Results may differ from the reference program's by a relative error of at most 0.0003.
Values sent between devices are 32-bit elements; how exact they have to be, the bound alone decides.
A program may use at most 64 MiB of HBM per device.

```python
import jax
import jax.numpy as jnp
from jax import lax

PW = 256
CB = 512
ROWS = 65536
COLS = 4096


def draw_matrix(key, part):
    subkeys = jax.random.split(jax.random.fold_in(key, 11), 5)
    position = jnp.arange(ROWS, dtype=jnp.float32) / ROWS
    rising = jnp.exp(0.5 * jnp.log(3.0) * position)
    roughness = jnp.exp(jax.random.uniform(subkeys[0], (ROWS,), minval=-1.15, maxval=1.15))
    row_scale = (rising * roughness)[:, None]
    col_scale = jnp.exp(jax.random.uniform(subkeys[1], (CB,), minval=-1.15, maxval=1.15))[None, :]
    entries = jax.random.truncated_normal(subkeys[2], -4.0, 4.0, (ROWS, CB))
    panel_cols = entries * col_scale * row_scale
    mixing = jax.random.normal(subkeys[3], (CB, COLS - CB)) / jnp.sqrt(float(CB))
    noise_part = jax.random.truncated_normal(subkeys[4], -4.0, 4.0, (ROWS, COLS - CB)) * row_scale
    trailing = jnp.dot(panel_cols, mixing, precision=lax.Precision.HIGHEST) + noise_part
    whole = jnp.concatenate([panel_cols, trailing], axis=1)
    return jnp.clip(whole, -80.0, 80.0).astype(jnp.float32)


def setup_inputs(seed: int = 0) -> dict:
    key_list = jax.random.split(jax.random.key(seed), 2)
    return {
        "matrix": draw_matrix(jax.random.fold_in(key_list[1], 71), 0),
    }


def inverse_factor(gram_matrix):
    factor_low = jnp.linalg.cholesky(gram_matrix)
    identity = jnp.eye(gram_matrix.shape[0], dtype=gram_matrix.dtype)
    return jax.scipy.linalg.solve_triangular(factor_low, identity, lower=True)

def reference(matrix):
    row_count = matrix.shape[0]
    remainder = matrix
    bases = []
    coeffs = []
    for panel_index in range(2):
        panel_cols = remainder[:, panel_index * PW:(panel_index + 1) * PW]
        gram_matrix = jnp.dot(panel_cols.T, panel_cols, precision=lax.Precision.HIGHEST) / row_count
        inverse = inverse_factor(gram_matrix)
        basis = jnp.dot(panel_cols, inverse.T, precision=lax.Precision.HIGHEST)
        coeff_part = jnp.dot(basis.T, remainder, precision=lax.Precision.HIGHEST) / row_count
        remainder = remainder - jnp.dot(basis, coeff_part, precision=lax.Precision.HIGHEST)
        bases.append(basis)
        coeffs.append(coeff_part)
    return (jnp.concatenate(bases, axis=1), jnp.concatenate(coeffs, axis=0), remainder)
```

```python
import functools

import jax
import jax.numpy as jnp
from jax import lax
from jax.experimental import pallas as pl
from jax.experimental.pallas import tpu as pltpu
from jax.sharding import PartitionSpec as P

MESH = pl.DeviceIdType.MESH
F32, BF16 = jnp.float32, jnp.bfloat16
X, Z, Y = 4, 8, 4
N, NB = 512, 128
CHUNKS = 4
SUBS = 8
PART = 256
BLOCKS = [(i, j) for j in range(4) for i in range(j, 4)]
GROUPS = 16 * len(BLOCKS)


def split(value):
    high = value.astype(BF16)
    return high, (value - high.astype(F32)).astype(BF16)


def dot3(left, right, dims):
    dot = functools.partial(
        lax.dot_general, dimension_numbers=(dims, ((), ())), preferred_element_type=F32
    )
    return dot(left[0], right[0]) + (dot(left[0], right[1]) + dot(left[1], right[0]))


def dot_full(left, right, dims):
    return lax.dot_general(
        left, right, (dims, ((), ())), precision=lax.Precision.HIGHEST, preferred_element_type=F32
    )


def leaf(tiles):
    lane = lax.broadcasted_iota(jnp.int32, (8, 128), 1)
    sub = lax.broadcasted_iota(jnp.int32, (8, 128), 0)
    tiles = list(tiles)
    for r in range(16):
        lo = 8 * r
        group = (lane >= lo) & (lane < lo + 8)
        cols = {
            i: [jnp.broadcast_to(tiles[i][:, lo + m : lo + m + 1], (8, 128)) for m in range(8)]
            for i in range(r, 16)
        }
        pivot = {
            (i, m): jnp.broadcast_to(cols[r][m][i : i + 1, :], (8, 128))
            for m in range(8)
            for i in range(m, 8)
        }
        base = jnp.where(group, (lane - lo == sub).astype(F32), tiles[r])
        rows = [jnp.broadcast_to(base[m : m + 1, :], (8, 128)) for m in range(8)]
        for i in range(r + 1, 16):
            tiles[i] = jnp.where(group, 0.0, tiles[i])
        out = jnp.zeros((8, 128), F32)
        for j in range(8):
            inv = lax.rsqrt(pivot[j, j])
            low = {m: pivot[m, j] * inv for m in range(j + 1, 8)}
            for m in range(j + 1, 8):
                for i in range(m, 8):
                    pivot[i, m] = pivot[i, m] - low[i] * low[m]
            row = rows[j] * inv
            for m in range(j + 1, 8):
                rows[m] = rows[m] - low[m] * row
            out = jnp.where(sub == j, row, out)
            for i in range(r + 1, 16):
                col = cols[i][j] * inv
                for m in range(j + 1, 8):
                    cols[i][m] = cols[i][m] - col * low[m]
                tiles[i] = tiles[i] - col * row
        tiles[r] = jnp.where(lane <= sub + lo, out, 0.0)
    return tiles


def factor(gram, inv):
    inv[...] = jnp.zeros_like(inv)
    for k in range(4):
        a, b = k * NB, (k + 1) * NB
        own = jnp.concatenate(leaf([gram[a + 8 * i : a + 8 * i + 8, a:b] for i in range(16)]), axis=0)
        inv[a:b, a:b] = own
        if k:
            inv[a:b, :a] = dot_full(own, inv[a:b, :a], ((1,), (0,)))
        if k < 3:
            low = dot_full(gram[b:, a:b], own, ((1,), (1,)))
            gram[b:, b:] = gram[b:, b:] - dot_full(low, low, ((1,), (1,)))
            inv[b:, :b] = inv[b:, :b] - dot_full(low, inv[a:b, :b], ((1,), (0,)))


def gather_kernel(
    rows_total, a_hbm, p_out, c_out, g_out,
    a, a_hi, a_lo, p, c_own, c_sib, c_x, c_s, c_z, c_all,
    g_own, g_sib, g_x, g_s, g_z, g_all,
    load_sem, store_sem, p_send, p_recv, cs_send, cs_recv, cx_send, cx_recv, cz_send, cz_recv,
    caz_send, caz_recv, cax_send, cax_recv, ce_send, ce_recv, gs_send, gs_recv, gx_send, gx_recv,
    gz_send, gz_recv, gy_send, gy_recv, gaz_send, gaz_recv, gax_send, gax_recv, ge_send, ge_recv,
):
    row, y = lax.axis_index("row"), lax.axis_index("col")
    core, z, x = row % 2, (row // 2) % Z, row // (2 * Z)
    piece = x * Z + z

    def at(px, py, pz, pc):
        return ((px * Z + pz) * 2 + pc, py)

    def x_peer(i):
        return (x + i) % X

    def z_peer(i):
        return (z + i) % Z

    def remote(src, dst, send, recv, device):
        return pltpu.make_async_remote_copy(
            src_ref=src, dst_ref=dst, send_sem=send, recv_sem=recv, device_id=device, device_id_type=MESH
        )

    sibling = at(x, y, z, 1 - core)
    barrier = pltpu.get_barrier_semaphore()
    friends = [sibling]
    friends += [at(x_peer(i), y, z, core) for i in range(1, X)]
    friends += [at(x, y, z_peer(i), core) for i in range(1, Z)]
    friends += [at(x, (y + i) % Y, z, core) for i in range(1, Y)]
    for friend in friends:
        pl.semaphore_signal(barrier, inc=1, device_id=friend, device_id_type=MESH)

    def p_copy(way, s, step):
        rows = pl.ds(512 * way + PART * (s % 2), PART)
        part = p.at[s // 2, rows, :]
        return remote(part, part, p_send.at[way, s], p_recv.at[way, s], at(x, (y + step) % Y, z, core))

    def up(s):
        return p_copy(0, s, 1)

    def down(s):
        return p_copy(1, s, Y - 1)

    def cs(k):
        return [remote(c_own.at[k], c_sib.at[k], cs_send.at[k], cs_recv.at[k], sibling)]

    def cx(k):
        return [
            remote(
                c_own.at[k, pl.ds(x_peer(i) * Z, Z)], c_x.at[k, i - 1],
                cx_send.at[k, i - 1], cx_recv.at[k, i - 1], at(x_peer(i), y, z, core),
            )
            for i in range(1, X)
        ]

    def cz(k):
        return [
            remote(
                c_s.at[k, z_peer(i)], c_z.at[k, i - 1],
                cz_send.at[k, i - 1], cz_recv.at[k, i - 1], at(x, y, z_peer(i), core),
            )
            for i in range(1, Z)
        ]

    def caz(k):
        return [
            remote(
                c_all.at[k, piece], c_all.at[k, piece],
                caz_send.at[k, i - 1], caz_recv.at[k, i - 1], at(x, y, z_peer(i), core),
            )
            for i in range(1, Z)
        ]

    def cax(k):
        own = c_all.at[k, pl.ds(x * Z, Z)]
        return [
            remote(own, own, cax_send.at[k, i - 1], cax_recv.at[k, i - 1], at(x_peer(i), y, z, core))
            for i in range(1, X)
        ]

    def ce(k):
        return [remote(c_all.at[k], c_all.at[k], ce_send.at[k], ce_recv.at[k], sibling)]

    five, forty = GROUPS // (X * Z), GROUPS // X

    def gs():
        return [remote(g_own, g_sib, gs_send, gs_recv, sibling)]

    def gx():
        return [
            remote(
                g_own.at[pl.ds(x_peer(i) * forty, forty)], g_x.at[i - 1],
                gx_send.at[i - 1], gx_recv.at[i - 1], at(x_peer(i), y, z, core),
            )
            for i in range(1, X)
        ]

    def gz():
        return [
            remote(
                g_s.at[pl.ds(z_peer(i) * five, five)], g_z.at[i - 1],
                gz_send.at[i - 1], gz_recv.at[i - 1], at(x, y, z_peer(i), core),
            )
            for i in range(1, Z)
        ]

    g_piece = g_all.at[pl.ds(piece * five, five)]

    def gy():
        return [
            remote(g_piece, g_piece, gy_send.at[i - 1], gy_recv, at(x, (y + i) % Y, z, core))
            for i in range(1, Y)
        ]

    def gaz():
        return [
            remote(g_piece, g_piece, gaz_send.at[i - 1], gaz_recv.at[i - 1], at(x, y, z_peer(i), core))
            for i in range(1, Z)
        ]

    def gax():
        own = g_all.at[pl.ds(x * forty, forty)]
        return [
            remote(own, own, gax_send.at[i - 1], gax_recv.at[i - 1], at(x_peer(i), y, z, core))
            for i in range(1, X)
        ]

    def ge():
        return [remote(g_all, g_all, ge_send, ge_recv, sibling)]

    def start(copies):
        for copy in copies:
            copy.start()

    def arrive(copies):
        for copy in copies:
            copy.wait_recv()

    def sent(copies):
        for copy in copies:
            copy.wait_send()

    def p_load(k):
        return pltpu.make_async_copy(a_hbm.at[:, pl.ds(NB * k, NB)], p.at[k], load_sem.at[1 + k])

    a_load = pltpu.make_async_copy(a_hbm, a, load_sem.at[0])

    @pl.when(y == 0)
    def _():
        for k in range(CHUNKS):
            p_load(k).start()

    a_load.start()

    @pl.when(y == 0)
    def _():
        for k in range(CHUNKS):
            p_load(k).wait()

    pl.semaphore_wait(barrier, len(friends))

    @pl.when(y == 0)
    def _():
        for s in range(SUBS):
            up(s).start()
            down(s).start()
        flipped = [split(p[k].T) for k in range(CHUNKS)]
        for b, (i, j) in enumerate(BLOCKS):
            block = dot3(flipped[i], flipped[j], ((1,), (1,)))
            for r in range(16):
                g_own[16 * b + r] = block[8 * r : 8 * r + 8, :]

        @pl.when(core == 0)
        def _():
            start(gs())

        @pl.when(core == 1)
        def _():
            arrive(gs())
            g_own[...] = g_own[...] + g_sib[...]
            start(gx())

    a_load.wait()
    for r in range(0, 1024, 256):
        high, low = split(a[r : r + 256, :])
        a_hi[r : r + 256, :] = high
        a_lo[r : r + 256, :] = low

    def p_step(t):
        @pl.when(y == 1)
        def _():
            if t < SUBS:
                up(t).wait_recv()
                up(t).start()
            if 0 <= t - 2 < SUBS:
                down(t - 2).wait_recv()

        @pl.when(y == 2)
        def _():
            if 0 <= t - 1 < SUBS:
                up(t - 1).wait_recv()
                up(t - 1).start()
                down(t - 1).wait_recv()
                down(t - 1).start()

        @pl.when(y == 3)
        def _():
            if t < SUBS:
                down(t).wait_recv()
                down(t).start()
            if 0 <= t - 2 < SUBS:
                up(t - 2).wait_recv()

    def p_store(k):
        return pltpu.make_async_copy(p.at[k], p_out.at[k], store_sem.at[k])

    def compute(k):
        left = split(p[k].T)
        for tile in range(4):
            lanes = slice(256 * tile, 256 * tile + 256)
            part = dot3(left, (a_hi[:, lanes], a_lo[:, lanes]), ((1,), (0,)))
            half, inner = tile // 2, slice(256 * (tile % 2), 256 * (tile % 2) + 256)
            for r in range(16):
                c_own[k, 2 * r + half, :, inner] = part[8 * r : 8 * r + 8, :]
        p_store(k).start()

    def c_stage(k, stage):
        if not 0 <= k < CHUNKS:
            return
        if stage == 1:
            arrive(cs(k))
            c_own[k] = c_own[k] + c_sib[k]
            start(cx(k))
        elif stage == 2:
            arrive(cx(k))
            c_s[k] = c_own[k, pl.ds(x * Z, Z)] + c_x[k, 0] + (c_x[k, 1] + c_x[k, 2])
            start(cz(k))
        elif stage == 3:
            arrive(cz(k))
            total = c_s[k, z]
            for i in range(Z - 1):
                total = total + c_z[k, i]
            c_all[k, piece] = total * (1.0 / rows_total)
            start(caz(k))
        elif stage == 4:
            arrive(caz(k))
            start(cax(k))
        elif stage == 5:
            arrive(cax(k))
            start(ce(k))

    def g_stage(t):
        if t == 4:

            @pl.when(y == 0)
            def _():
                arrive(gx())
                g_s[...] = g_own[pl.ds(x * forty, forty)] + g_x[0] + (g_x[1] + g_x[2])
                start(gz())

        if t == 6:

            @pl.when(y == 0)
            def _():
                arrive(gz())
                total = g_s[pl.ds(z * five, five)]
                for i in range(Z - 1):
                    total = total + g_z[i]
                g_all[pl.ds(piece * five, five)] = total * (1.0 / rows_total)
                start(gy())

        if t == 8:

            @pl.when(y != 0)
            def _():
                gy()[0].wait_recv()

            start(gaz())
        if t == 10:
            arrive(gaz())
            start(gax())
        if t == 12:
            arrive(gax())
            start(ge())

    for t in range(14):
        p_step(t)
        ready = (t - 3) // 2
        fresh = t >= 3 and t % 2 == 1 and ready < CHUNKS
        if fresh:
            compute(ready)

        @pl.when(core == 1)
        def _():
            if fresh:
                start(cs(ready))
            g_stage(t)

        @pl.when(core == 0)
        def _():
            if fresh:
                c_stage(ready, 1)
            for stage in range(5, 1, -1):
                if (t - stage - 2) % 2 == 0:
                    c_stage((t - stage - 2) // 2, stage)

    g_store = pltpu.make_async_copy(g_all, g_out, store_sem.at[4])

    def c_store(k):
        return pltpu.make_async_copy(c_all.at[k], c_out.at[k], store_sem.at[5 + k])

    @pl.when(core == 0)
    def _():
        for k in range(CHUNKS):
            c_store(k).start()
        arrive(ge())
        g_store.start()

    @pl.when(core == 1)
    def _():
        g_store.start()
        for k in range(CHUNKS):
            arrive(ce(k))
            c_store(k).start()

    @pl.when((y == 0) | (y == 1) | (y == 2))
    def _():
        for s in range(SUBS):
            up(s).wait_send()

    @pl.when((y == 0) | (y == 2) | (y == 3))
    def _():
        for s in range(SUBS):
            down(s).wait_send()

    @pl.when(core == 0)
    def _():
        @pl.when(y == 0)
        def _():
            sent(gs())

        for k in range(CHUNKS):
            sent(cx(k) + cz(k) + caz(k) + cax(k) + ce(k))

    @pl.when(core == 1)
    def _():
        @pl.when(y == 0)
        def _():
            sent(gx() + gz() + gy())

        for k in range(CHUNKS):
            sent(cs(k))
        sent(gaz() + gax() + ge())

    for k in range(CHUNKS):
        p_store(k).wait()
        c_store(k).wait()
    g_store.wait()


def factor_kernel(groups, inv, gram):
    for b, (i, j) in enumerate(BLOCKS):
        for r in range(16):
            gram[NB * i + 8 * r : NB * i + 8 * r + 8, NB * j : NB * j + NB] = groups[16 * b + r]
    factor(gram, inv)


def finish_kernel(a, p, inv, c, q, coeff, rest, inv_hi, inv_lo, coeff_hi, coeff_lo):
    half = N // 2

    @pl.when(pl.program_id(0) == 0)
    def _():
        high, low = split(inv[...])
        inv_hi[...] = high
        inv_lo[...] = low
        for tile in range(2):
            lanes = slice(512 * tile, 512 * tile + 512)
            sums = [
                jnp.concatenate([c[k, 2 * r + tile] for k in ks for r in range(16)], axis=0)
                for ks in ((0, 1), (2, 3))
            ]
            right = split(jnp.concatenate(sums, axis=0))
            upper = dot3(
                (high[:half, :half], low[:half, :half]), (right[0][:half], right[1][:half]), ((1,), (0,))
            )
            lower = dot3((high[half:], low[half:]), right, ((1,), (0,)))
            for start, part in ((0, upper), (half, lower)):
                coeff[start : start + half, lanes] = part
                part_hi, part_lo = split(part)
                coeff_hi[start : start + half, lanes] = part_hi
                coeff_lo[start : start + half, lanes] = part_lo

    panels = split(jnp.concatenate([p[k] for k in range(CHUNKS)], axis=1))
    upper = dot3(
        (panels[0][:, :half], panels[1][:, :half]),
        (inv_hi[:half, :half], inv_lo[:half, :half]),
        ((1,), (1,)),
    )
    lower = dot3(panels, (inv_hi[half:, :], inv_lo[half:, :]), ((1,), (1,)))
    basis = jnp.concatenate([upper, lower], axis=1)
    q[...] = basis
    left = split(basis)
    for tile in range(2):
        lanes = slice(512 * tile, 512 * tile + 512)
        rest[:, lanes] = a[:, lanes] - dot3(left, (coeff_hi[:, lanes], coeff_lo[:, lanes]), ((1,), (0,)))


def vmem(*shape, dtype=F32):
    return pltpu.VMEM(shape, dtype)


def dma(*shape):
    return pltpu.SemaphoreType.DMA(shape) if shape else pltpu.SemaphoreType.DMA


def on_device(matrix):
    rows_total = matrix.shape[0] * lax.axis_size("row")
    any_space = pl.BlockSpec(memory_space=pl.ANY)
    five, forty = GROUPS // (X * Z), GROUPS // X
    pairs = [
        (2, SUBS), (4,), (4, 3), (4, 7), (4, 7), (4, 3), (4,), (), (3,), (7,),
    ]
    sems = [dma(*shape) for shape in pairs for _ in range(2)]
    panels, sums, groups = pl.pallas_call(
        functools.partial(gather_kernel, rows_total),
        out_shape=(
            jax.ShapeDtypeStruct((4, 1024, NB), F32),
            jax.ShapeDtypeStruct((4, 32, 8, 512), F32),
            jax.ShapeDtypeStruct((GROUPS, 8, 128), F32),
        ),
        in_specs=[any_space],
        out_specs=[any_space] * 3,
        scratch_shapes=[
            vmem(1024, 1024), vmem(1024, 1024, dtype=BF16), vmem(1024, 1024, dtype=BF16),
            vmem(4, 1024, NB), vmem(4, 32, 8, 512), vmem(4, 32, 8, 512), vmem(4, 3, 8, 8, 512),
            vmem(4, 8, 8, 512), vmem(4, 7, 8, 512), vmem(4, 32, 8, 512),
            vmem(GROUPS, 8, 128), vmem(GROUPS, 8, 128), vmem(3, forty, 8, 128), vmem(forty, 8, 128),
            vmem(7, five, 8, 128), vmem(GROUPS, 8, 128),
            dma(5), dma(9), *sems,
            dma(3), dma(), dma(7), dma(7), dma(3), dma(3), dma(), dma(),
        ],
        compiler_params=pltpu.CompilerParams(
            collective_id=0, has_side_effects=True, vmem_limit_bytes=56 * 1024 * 1024
        ),
        name="gather",
    )(matrix)
    inverse = pl.pallas_call(
        factor_kernel,
        out_shape=jax.ShapeDtypeStruct((N, N), F32),
        in_specs=[pl.BlockSpec(memory_space=pltpu.VMEM)],
        out_specs=pl.BlockSpec(memory_space=pltpu.VMEM),
        scratch_shapes=[vmem(N, N)],
        compiler_params=pltpu.CompilerParams(vmem_limit_bytes=32 * 1024 * 1024),
        name="factor",
    )(groups)
    tile = 256
    return pl.pallas_call(
        finish_kernel,
        grid=(1024 // tile,),
        out_shape=(
            jax.ShapeDtypeStruct((1024, N), F32),
            jax.ShapeDtypeStruct((N, 1024), F32),
            jax.ShapeDtypeStruct((1024, 1024), F32),
        ),
        in_specs=[
            pl.BlockSpec((tile, 1024), lambda i: (i, 0)),
            pl.BlockSpec((4, tile, NB), lambda i: (0, i, 0)),
            pl.BlockSpec((N, N), lambda i: (0, 0)),
            pl.BlockSpec((4, 32, 8, 512), lambda i: (0, 0, 0, 0)),
        ],
        out_specs=[
            pl.BlockSpec((tile, N), lambda i: (i, 0)),
            pl.BlockSpec((N, 1024), lambda i: (0, 0)),
            pl.BlockSpec((tile, 1024), lambda i: (i, 0)),
        ],
        scratch_shapes=[
            vmem(N, N, dtype=BF16), vmem(N, N, dtype=BF16),
            vmem(N, 1024, dtype=BF16), vmem(N, 1024, dtype=BF16),
        ],
        compiler_params=pltpu.CompilerParams(vmem_limit_bytes=48 * 1024 * 1024),
        name="finish",
    )(matrix, panels, inverse, sums)


def solution(mesh):
    return jax.shard_map(
        on_device,
        mesh=mesh,
        in_specs=(P("row", "col"),),
        out_specs=(P("row", None), P(None, "col"), P("row", "col")),
        check_vma=False,
    )
```

```python
import functools

import jax
import jax.numpy as jnp
from jax import lax
from jax.experimental import pallas as pl
from jax.experimental.pallas import tpu as pltpu
from jax.sharding import PartitionSpec as P

MESH = pl.DeviceIdType.MESH
F32, BF16 = jnp.float32, jnp.bfloat16
X, Z, Y = 4, 8, 4
N, NB = 512, 128
CHUNKS = 4
SUBS = 8
PART = 256
BLOCKS = [(i, j) for j in range(4) for i in range(j, 4)]
GROUPS = 16 * len(BLOCKS)


def split(value):
    high = value.astype(BF16)
    return high, (value - high.astype(F32)).astype(BF16)


def dot3(left, right, dims):
    dot = functools.partial(
        lax.dot_general, dimension_numbers=(dims, ((), ())), preferred_element_type=F32
    )
    return dot(left[0], right[0]) + (dot(left[0], right[1]) + dot(left[1], right[0]))


def dot_full(left, right, dims):
    return lax.dot_general(
        left, right, (dims, ((), ())), precision=lax.Precision.HIGHEST, preferred_element_type=F32
    )


def leaf(tiles):
    lane = lax.broadcasted_iota(jnp.int32, (8, 128), 1)
    sub = lax.broadcasted_iota(jnp.int32, (8, 128), 0)
    tiles = list(tiles)
    for r in range(16):
        lo = 8 * r
        group = (lane >= lo) & (lane < lo + 8)
        cols = {
            i: [jnp.broadcast_to(tiles[i][:, lo + m : lo + m + 1], (8, 128)) for m in range(8)]
            for i in range(r, 16)
        }
        pivot = {
            (i, m): jnp.broadcast_to(cols[r][m][i : i + 1, :], (8, 128))
            for m in range(8)
            for i in range(m, 8)
        }
        base = jnp.where(group, (lane - lo == sub).astype(F32), tiles[r])
        rows = [jnp.broadcast_to(base[m : m + 1, :], (8, 128)) for m in range(8)]
        for i in range(r + 1, 16):
            tiles[i] = jnp.where(group, 0.0, tiles[i])
        out = jnp.zeros((8, 128), F32)
        for j in range(8):
            inv = lax.rsqrt(pivot[j, j])
            low = {m: pivot[m, j] * inv for m in range(j + 1, 8)}
            for m in range(j + 1, 8):
                for i in range(m, 8):
                    pivot[i, m] = pivot[i, m] - low[i] * low[m]
            row = rows[j] * inv
            for m in range(j + 1, 8):
                rows[m] = rows[m] - low[m] * row
            out = jnp.where(sub == j, row, out)
            for i in range(r + 1, 16):
                col = cols[i][j] * inv
                for m in range(j + 1, 8):
                    cols[i][m] = cols[i][m] - col * low[m]
                tiles[i] = tiles[i] - col * row
        tiles[r] = jnp.where(lane <= sub + lo, out, 0.0)
    return tiles


def factor(gram, inv, done):
    inv[...] = jnp.zeros_like(inv)
    for k in range(4):
        a, b = k * NB, (k + 1) * NB
        own = jnp.concatenate(leaf([gram[a + 8 * i : a + 8 * i + 8, a:b] for i in range(16)]), axis=0)
        inv[a:b, a:b] = own
        if k:
            inv[a:b, :a] = dot_full(own, inv[a:b, :a], ((1,), (0,)))
        done(k)
        if k < 3:
            low = dot_full(gram[b:, a:b], own, ((1,), (1,)))
            gram[b:, b:] = gram[b:, b:] - dot_full(low, low, ((1,), (1,)))
            inv[b:, :b] = inv[b:, :b] - dot_full(low, inv[a:b, :b], ((1,), (0,)))


def gather_kernel(
    rows_total, a_hbm, p_out, c_out, inv_out,
    a, a_hi, a_lo, p, c_own, c_sib, c_x, c_s, c_z, c_all,
    g_own, g_sib, g_x, g_s, g_z, g_all, gram, inv,
    load_sem, store_sem, p_send, p_recv, cs_send, cs_recv, cx_send, cx_recv, cz_send, cz_recv,
    caz_send, caz_recv, cax_send, cax_recv, ce_send, ce_recv, gs_send, gs_recv, gx_send, gx_recv,
    gz_send, gz_recv, gy_send, gy_recv, gaz_send, gaz_recv, gax_send, gax_recv, ge_send, ge_recv,
):
    row, y = lax.axis_index("row"), lax.axis_index("col")
    core, z, x = row % 2, (row // 2) % Z, row // (2 * Z)
    piece = x * Z + z

    def at(px, py, pz, pc):
        return ((px * Z + pz) * 2 + pc, py)

    def x_peer(i):
        return (x + i) % X

    def z_peer(i):
        return (z + i) % Z

    def remote(src, dst, send, recv, device):
        return pltpu.make_async_remote_copy(
            src_ref=src, dst_ref=dst, send_sem=send, recv_sem=recv, device_id=device, device_id_type=MESH
        )

    sibling = at(x, y, z, 1 - core)
    barrier = pltpu.get_barrier_semaphore()
    friends = [sibling]
    friends += [at(x_peer(i), y, z, core) for i in range(1, X)]
    friends += [at(x, y, z_peer(i), core) for i in range(1, Z)]
    friends += [at(x, (y + i) % Y, z, core) for i in range(1, Y)]
    for friend in friends:
        pl.semaphore_signal(barrier, inc=1, device_id=friend, device_id_type=MESH)

    def p_copy(way, s, step):
        rows = pl.ds(512 * way + PART * (s % 2), PART)
        part = p.at[s // 2, rows, :]
        return remote(part, part, p_send.at[way, s], p_recv.at[way, s], at(x, (y + step) % Y, z, core))

    def up(s):
        return p_copy(0, s, 1)

    def down(s):
        return p_copy(1, s, Y - 1)

    def cs(k):
        return [remote(c_own.at[k], c_sib.at[k], cs_send.at[k], cs_recv.at[k], sibling)]

    def cx(k):
        return [
            remote(
                c_own.at[k, pl.ds(x_peer(i) * Z, Z)], c_x.at[k, i - 1],
                cx_send.at[k, i - 1], cx_recv.at[k, i - 1], at(x_peer(i), y, z, core),
            )
            for i in range(1, X)
        ]

    def cz(k):
        return [
            remote(
                c_s.at[k, z_peer(i)], c_z.at[k, i - 1],
                cz_send.at[k, i - 1], cz_recv.at[k, i - 1], at(x, y, z_peer(i), core),
            )
            for i in range(1, Z)
        ]

    def caz(k):
        return [
            remote(
                c_all.at[k, piece], c_all.at[k, piece],
                caz_send.at[k, i - 1], caz_recv.at[k, i - 1], at(x, y, z_peer(i), core),
            )
            for i in range(1, Z)
        ]

    def cax(k):
        own = c_all.at[k, pl.ds(x * Z, Z)]
        return [
            remote(own, own, cax_send.at[k, i - 1], cax_recv.at[k, i - 1], at(x_peer(i), y, z, core))
            for i in range(1, X)
        ]

    def ce(k):
        return [remote(c_all.at[k], c_all.at[k], ce_send.at[k], ce_recv.at[k], sibling)]

    five, forty = GROUPS // (X * Z), GROUPS // X

    def gs():
        return [remote(g_own, g_sib, gs_send, gs_recv, sibling)]

    def gx():
        return [
            remote(
                g_own.at[pl.ds(x_peer(i) * forty, forty)], g_x.at[i - 1],
                gx_send.at[i - 1], gx_recv.at[i - 1], at(x_peer(i), y, z, core),
            )
            for i in range(1, X)
        ]

    def gz():
        return [
            remote(
                g_s.at[pl.ds(z_peer(i) * five, five)], g_z.at[i - 1],
                gz_send.at[i - 1], gz_recv.at[i - 1], at(x, y, z_peer(i), core),
            )
            for i in range(1, Z)
        ]

    g_piece = g_all.at[pl.ds(piece * five, five)]

    def gy():
        return [
            remote(g_piece, g_piece, gy_send.at[i - 1], gy_recv, at(x, (y + i) % Y, z, core))
            for i in range(1, Y)
        ]

    def gaz():
        return [
            remote(g_piece, g_piece, gaz_send.at[i - 1], gaz_recv.at[i - 1], at(x, y, z_peer(i), core))
            for i in range(1, Z)
        ]

    def gax():
        own = g_all.at[pl.ds(x * forty, forty)]
        return [
            remote(own, own, gax_send.at[i - 1], gax_recv.at[i - 1], at(x_peer(i), y, z, core))
            for i in range(1, X)
        ]

    def ge(k):
        rows = inv.at[pl.ds(NB * k, NB)]
        return [remote(rows, rows, ge_send.at[k], ge_recv.at[k], sibling)]

    def start(copies):
        for copy in copies:
            copy.start()

    def arrive(copies):
        for copy in copies:
            copy.wait_recv()

    def sent(copies):
        for copy in copies:
            copy.wait_send()

    def p_load(k):
        return pltpu.make_async_copy(a_hbm.at[:, pl.ds(NB * k, NB)], p.at[k], load_sem.at[1 + k])

    a_load = pltpu.make_async_copy(a_hbm, a, load_sem.at[0])

    @pl.when(y == 0)
    def _():
        for k in range(CHUNKS):
            p_load(k).start()

    a_load.start()

    @pl.when(y == 0)
    def _():
        for k in range(CHUNKS):
            p_load(k).wait()

    pl.semaphore_wait(barrier, len(friends))

    @pl.when(y == 0)
    def _():
        for s in range(SUBS):
            up(s).start()
            down(s).start()
        flipped = [split(p[k].T) for k in range(CHUNKS)]
        for b, (i, j) in enumerate(BLOCKS):
            block = dot3(flipped[i], flipped[j], ((1,), (1,)))
            for r in range(16):
                g_own[16 * b + r] = block[8 * r : 8 * r + 8, :]

        @pl.when(core == 0)
        def _():
            start(gs())

        @pl.when(core == 1)
        def _():
            arrive(gs())
            g_own[...] = g_own[...] + g_sib[...]
            start(gx())

    a_load.wait()
    for r in range(0, 1024, 256):
        high, low = split(a[r : r + 256, :])
        a_hi[r : r + 256, :] = high
        a_lo[r : r + 256, :] = low

    def p_step(t):
        @pl.when(y == 1)
        def _():
            if t < SUBS:
                up(t).wait_recv()
                up(t).start()
            if 0 <= t - 2 < SUBS:
                down(t - 2).wait_recv()

        @pl.when(y == 2)
        def _():
            if 0 <= t - 1 < SUBS:
                up(t - 1).wait_recv()
                up(t - 1).start()
                down(t - 1).wait_recv()
                down(t - 1).start()

        @pl.when(y == 3)
        def _():
            if t < SUBS:
                down(t).wait_recv()
                down(t).start()
            if 0 <= t - 2 < SUBS:
                up(t - 2).wait_recv()

    def p_store(k):
        return pltpu.make_async_copy(p.at[k], p_out.at[k], store_sem.at[k])

    def compute(k):
        left = split(p[k].T)
        for tile in range(4):
            lanes = slice(256 * tile, 256 * tile + 256)
            part = dot3(left, (a_hi[:, lanes], a_lo[:, lanes]), ((1,), (0,)))
            half, inner = tile // 2, slice(256 * (tile % 2), 256 * (tile % 2) + 256)
            for r in range(16):
                c_own[k, 2 * r + half, :, inner] = part[8 * r : 8 * r + 8, :]
        p_store(k).start()

    def c_stage(k, stage):
        if not 0 <= k < CHUNKS:
            return
        if stage == 1:
            arrive(cs(k))
            c_own[k] = c_own[k] + c_sib[k]
            start(cx(k))
        elif stage == 2:
            arrive(cx(k))
            c_s[k] = c_own[k, pl.ds(x * Z, Z)] + c_x[k, 0] + (c_x[k, 1] + c_x[k, 2])
            start(cz(k))
        elif stage == 3:
            arrive(cz(k))
            total = c_s[k, z]
            for i in range(Z - 1):
                total = total + c_z[k, i]
            c_all[k, piece] = total * (1.0 / rows_total)
            start(caz(k))
        elif stage == 4:
            arrive(caz(k))
            start(cax(k))
        elif stage == 5:
            arrive(cax(k))
            start(ce(k))

    def g_stage(t):
        if t == 4:

            @pl.when(y == 0)
            def _():
                arrive(gx())
                g_s[...] = g_own[pl.ds(x * forty, forty)] + g_x[0] + (g_x[1] + g_x[2])
                start(gz())

        if t == 6:

            @pl.when(y == 0)
            def _():
                arrive(gz())
                total = g_s[pl.ds(z * five, five)]
                for i in range(Z - 1):
                    total = total + g_z[i]
                g_all[pl.ds(piece * five, five)] = total * (1.0 / rows_total)
                start(gy())

        if t == 8:

            @pl.when(y != 0)
            def _():
                gy()[0].wait_recv()

            start(gaz())
        if t == 10:
            arrive(gaz())
            start(gax())
        if t == 12:
            arrive(gax())
            for b, (i, j) in enumerate(BLOCKS):
                for r in range(16):
                    gram[NB * i + 8 * r : NB * i + 8 * r + 8, NB * j : NB * j + NB] = g_all[16 * b + r]
            factor(gram, inv, lambda k: start(ge(k)))

    for t in range(14):
        p_step(t)
        ready = (t - 3) // 2
        fresh = t >= 3 and t % 2 == 1 and ready < CHUNKS
        if fresh:
            compute(ready)

        @pl.when(core == 1)
        def _():
            if fresh:
                start(cs(ready))
            g_stage(t)

        @pl.when(core == 0)
        def _():
            if fresh:
                c_stage(ready, 1)
            for stage in range(5, 1, -1):
                if (t - stage - 2) % 2 == 0:
                    c_stage((t - stage - 2) // 2, stage)

    inv_store = pltpu.make_async_copy(inv, inv_out, store_sem.at[4])

    def c_store(k):
        return pltpu.make_async_copy(c_all.at[k], c_out.at[k], store_sem.at[5 + k])

    @pl.when(core == 0)
    def _():
        for k in range(CHUNKS):
            c_store(k).start()
        for k in range(4):
            arrive(ge(k))
        inv_store.start()

    @pl.when(core == 1)
    def _():
        inv_store.start()
        for k in range(CHUNKS):
            arrive(ce(k))
            c_store(k).start()

    @pl.when((y == 0) | (y == 1) | (y == 2))
    def _():
        for s in range(SUBS):
            up(s).wait_send()

    @pl.when((y == 0) | (y == 2) | (y == 3))
    def _():
        for s in range(SUBS):
            down(s).wait_send()

    @pl.when(core == 0)
    def _():
        @pl.when(y == 0)
        def _():
            sent(gs())

        for k in range(CHUNKS):
            sent(cx(k) + cz(k) + caz(k) + cax(k) + ce(k))

    @pl.when(core == 1)
    def _():
        @pl.when(y == 0)
        def _():
            sent(gx() + gz() + gy())

        for k in range(CHUNKS):
            sent(cs(k))
            sent(ge(k))
        sent(gaz() + gax())

    for k in range(CHUNKS):
        p_store(k).wait()
        c_store(k).wait()
    inv_store.wait()


def finish_kernel(a, p, inv, c, q, coeff, rest, inv_hi, inv_lo, coeff_hi, coeff_lo):
    half = N // 2

    @pl.when(pl.program_id(0) == 0)
    def _():
        high, low = split(inv[...])
        inv_hi[...] = high
        inv_lo[...] = low
        for tile in range(2):
            lanes = slice(512 * tile, 512 * tile + 512)
            sums = [
                jnp.concatenate([c[k, 2 * r + tile] for k in ks for r in range(16)], axis=0)
                for ks in ((0, 1), (2, 3))
            ]
            right = split(jnp.concatenate(sums, axis=0))
            upper = dot3(
                (high[:half, :half], low[:half, :half]), (right[0][:half], right[1][:half]), ((1,), (0,))
            )
            lower = dot3((high[half:], low[half:]), right, ((1,), (0,)))
            for start, part in ((0, upper), (half, lower)):
                coeff[start : start + half, lanes] = part
                part_hi, part_lo = split(part)
                coeff_hi[start : start + half, lanes] = part_hi
                coeff_lo[start : start + half, lanes] = part_lo

    panels = split(jnp.concatenate([p[k] for k in range(CHUNKS)], axis=1))
    upper = dot3(
        (panels[0][:, :half], panels[1][:, :half]),
        (inv_hi[:half, :half], inv_lo[:half, :half]),
        ((1,), (1,)),
    )
    lower = dot3(panels, (inv_hi[half:, :], inv_lo[half:, :]), ((1,), (1,)))
    basis = jnp.concatenate([upper, lower], axis=1)
    q[...] = basis
    left = split(basis)
    for tile in range(2):
        lanes = slice(512 * tile, 512 * tile + 512)
        rest[:, lanes] = a[:, lanes] - dot3(left, (coeff_hi[:, lanes], coeff_lo[:, lanes]), ((1,), (0,)))


def vmem(*shape, dtype=F32):
    return pltpu.VMEM(shape, dtype)


def dma(*shape):
    return pltpu.SemaphoreType.DMA(shape) if shape else pltpu.SemaphoreType.DMA


def on_device(matrix):
    rows_total = matrix.shape[0] * lax.axis_size("row")
    any_space = pl.BlockSpec(memory_space=pl.ANY)
    five, forty = GROUPS // (X * Z), GROUPS // X
    pairs = [
        (2, SUBS), (4,), (4, 3), (4, 7), (4, 7), (4, 3), (4,), (), (3,), (7,),
    ]
    sems = [dma(*shape) for shape in pairs for _ in range(2)]
    panels, sums, inverse = pl.pallas_call(
        functools.partial(gather_kernel, rows_total),
        out_shape=(
            jax.ShapeDtypeStruct((4, 1024, NB), F32),
            jax.ShapeDtypeStruct((4, 32, 8, 512), F32),
            jax.ShapeDtypeStruct((N, N), F32),
        ),
        in_specs=[any_space],
        out_specs=[any_space] * 3,
        scratch_shapes=[
            vmem(1024, 1024), vmem(1024, 1024, dtype=BF16), vmem(1024, 1024, dtype=BF16),
            vmem(4, 1024, NB), vmem(4, 32, 8, 512), vmem(4, 32, 8, 512), vmem(4, 3, 8, 8, 512),
            vmem(4, 8, 8, 512), vmem(4, 7, 8, 512), vmem(4, 32, 8, 512),
            vmem(GROUPS, 8, 128), vmem(GROUPS, 8, 128), vmem(3, forty, 8, 128), vmem(forty, 8, 128),
            vmem(7, five, 8, 128), vmem(GROUPS, 8, 128), vmem(N, N), vmem(N, N),
            dma(5), dma(9), *sems,
            dma(3), dma(), dma(7), dma(7), dma(3), dma(3), dma(4), dma(4),
        ],
        compiler_params=pltpu.CompilerParams(
            collective_id=0, has_side_effects=True, vmem_limit_bytes=56 * 1024 * 1024
        ),
        name="gather",
    )(matrix)
    tile = 256
    return pl.pallas_call(
        finish_kernel,
        grid=(1024 // tile,),
        out_shape=(
            jax.ShapeDtypeStruct((1024, N), F32),
            jax.ShapeDtypeStruct((N, 1024), F32),
            jax.ShapeDtypeStruct((1024, 1024), F32),
        ),
        in_specs=[
            pl.BlockSpec((tile, 1024), lambda i: (i, 0)),
            pl.BlockSpec((4, tile, NB), lambda i: (0, i, 0)),
            pl.BlockSpec((N, N), lambda i: (0, 0)),
            pl.BlockSpec((4, 32, 8, 512), lambda i: (0, 0, 0, 0)),
        ],
        out_specs=[
            pl.BlockSpec((tile, N), lambda i: (i, 0)),
            pl.BlockSpec((N, 1024), lambda i: (0, 0)),
            pl.BlockSpec((tile, 1024), lambda i: (i, 0)),
        ],
        scratch_shapes=[
            vmem(N, N, dtype=BF16), vmem(N, N, dtype=BF16),
            vmem(N, 1024, dtype=BF16), vmem(N, 1024, dtype=BF16),
        ],
        compiler_params=pltpu.CompilerParams(vmem_limit_bytes=60 * 1024 * 1024),
        name="finish",
    )(matrix, panels, inverse, sums)


def solution(mesh):
    return jax.shard_map(
        on_device,
        mesh=mesh,
        in_specs=(P("row", "col"),),
        out_specs=(P("row", None), P(None, "col"), P("row", "col")),
        check_vma=False,
    )
```

```python
import functools

import jax
import jax.numpy as jnp
from jax import lax
from jax.experimental import pallas as pl
from jax.experimental.pallas import tpu as pltpu
from jax.sharding import PartitionSpec as P

MESH = pl.DeviceIdType.MESH
F32, BF16 = jnp.float32, jnp.bfloat16
X, Z, Y = 4, 8, 4
N, NB = 512, 128
STEP = 32
SUBS = N // STEP
MID, END = 2, 5
WIDTHS = (128, 128, 128, 64, 64)
CHUNKS = len(WIDTHS)
STARTS = [sum(WIDTHS[:k]) for k in range(CHUNKS)]
READY = [(STARTS[k] + WIDTHS[k]) // STEP - 1 + END for k in range(CHUNKS)]
SPACING = 4
BLOCKS = [(i, j) for j in range(4) for i in range(j, 4)]
GROUPS = 16 * len(BLOCKS)


def split(value):
    high = value.astype(BF16)
    return high, (value - high.astype(F32)).astype(BF16)


def dot3(left, right, dims):
    dot = functools.partial(
        lax.dot_general, dimension_numbers=(dims, ((), ())), preferred_element_type=F32
    )
    return dot(left[0], right[0]) + (dot(left[0], right[1]) + dot(left[1], right[0]))


def dot_full(left, right, dims):
    return lax.dot_general(
        left, right, (dims, ((), ())), precision=lax.Precision.HIGHEST, preferred_element_type=F32
    )


def leaf(tiles):
    lane = lax.broadcasted_iota(jnp.int32, (8, 128), 1)
    sub = lax.broadcasted_iota(jnp.int32, (8, 128), 0)
    tiles = list(tiles)
    for r in range(16):
        lo = 8 * r
        group = (lane >= lo) & (lane < lo + 8)
        cols = {
            i: [jnp.broadcast_to(tiles[i][:, lo + m : lo + m + 1], (8, 128)) for m in range(8)]
            for i in range(r, 16)
        }
        pivot = {
            (i, m): jnp.broadcast_to(cols[r][m][i : i + 1, :], (8, 128))
            for m in range(8)
            for i in range(m, 8)
        }
        base = jnp.where(group, (lane - lo == sub).astype(F32), tiles[r])
        rows = [jnp.broadcast_to(base[m : m + 1, :], (8, 128)) for m in range(8)]
        for i in range(r + 1, 16):
            tiles[i] = jnp.where(group, 0.0, tiles[i])
        out = jnp.zeros((8, 128), F32)
        for j in range(8):
            inv = lax.rsqrt(pivot[j, j])
            low = {m: pivot[m, j] * inv for m in range(j + 1, 8)}
            for m in range(j + 1, 8):
                for i in range(m, 8):
                    pivot[i, m] = pivot[i, m] - low[i] * low[m]
            row = rows[j] * inv
            for m in range(j + 1, 8):
                rows[m] = rows[m] - low[m] * row
            out = jnp.where(sub == j, row, out)
            for i in range(r + 1, 16):
                col = cols[i][j] * inv
                for m in range(j + 1, 8):
                    cols[i][m] = cols[i][m] - col * low[m]
                tiles[i] = tiles[i] - col * row
        tiles[r] = jnp.where(lane <= sub + lo, out, 0.0)
    return tiles


def factor(gram, inv, done):
    inv[...] = jnp.zeros_like(inv)
    for k in range(4):
        a, b = k * NB, (k + 1) * NB
        own = jnp.concatenate(leaf([gram[a + 8 * i : a + 8 * i + 8, a:b] for i in range(16)]), axis=0)
        inv[a:b, a:b] = own
        if k:
            inv[a:b, :a] = dot_full(own, inv[a:b, :a], ((1,), (0,)))
        done(k)
        if k < 3:
            low = dot_full(gram[b:, a:b], own, ((1,), (1,)))
            gram[b:, b:] = gram[b:, b:] - dot_full(low, low, ((1,), (1,)))
            inv[b:, :b] = inv[b:, :b] - dot_full(low, inv[a:b, :b], ((1,), (0,)))


def gather_kernel(rows_total, a_hbm, q_out, coeff_out, *scratch):
    scratch = list(scratch)

    def take(count):
        taken = scratch[:count]
        del scratch[:count]
        return taken

    a, a_hi, a_lo, p, c_full, q, coeff = take(7)
    c_own, c_sib, c_x, c_s, c_z, c_all = (take(CHUNKS) for _ in range(6))
    g_own, g_sib, g_x, g_s, g_z, g_all, gram, inv = take(8)
    load_sem, store_sem, p_send, p_recv, cs_send, cs_recv, cx_send, cx_recv, cz_send, cz_recv = take(10)
    caz_send, caz_recv, cax_send, cax_recv, ce_send, ce_recv, gs_send, gs_recv, gx_send, gx_recv = take(10)
    gz_send, gz_recv, gy_send, gy_recv, gaz_send, gaz_recv, gax_send, gax_recv, ge_send, ge_recv = take(10)
    row, y = lax.axis_index("row"), lax.axis_index("col")
    core, z, x = row % 2, (row // 2) % Z, row // (2 * Z)
    piece = x * Z + z

    def at(px, py, pz, pc):
        return ((px * Z + pz) * 2 + pc, py)

    def x_peer(i):
        return (x + i) % X

    def z_peer(i):
        return (z + i) % Z

    def remote(src, dst, send, recv, device):
        return pltpu.make_async_remote_copy(
            src_ref=src, dst_ref=dst, send_sem=send, recv_sem=recv, device_id=device, device_id_type=MESH
        )

    sibling = at(x, y, z, 1 - core)
    barrier = pltpu.get_barrier_semaphore()
    friends = [sibling]
    friends += [at(x_peer(i), y, z, core) for i in range(1, X)]
    friends += [at(x, y, z_peer(i), core) for i in range(1, Z)]
    friends += [at(x, (y + i) % Y, z, core) for i in range(1, Y)]
    for friend in friends:
        pl.semaphore_signal(barrier, inc=1, device_id=friend, device_id_type=MESH)

    def p_copy(way, s, step):
        part = p.at[way, pl.ds(STEP * s, STEP)]
        return remote(part, part, p_send.at[way, s], p_recv.at[way, s], at(x, (y + step) % Y, z, core))

    def up(s):
        return p_copy(0, s, 1)

    def down(s):
        return p_copy(1, s, Y - 1)

    def cs(k):
        return [remote(c_own[k], c_sib[k], cs_send.at[k], cs_recv.at[k], sibling)]

    def cx(k):
        return [
            remote(
                c_own[k].at[pl.ds(x_peer(i) * Z, Z)], c_x[k].at[i - 1],
                cx_send.at[k, i - 1], cx_recv.at[k, i - 1], at(x_peer(i), y, z, core),
            )
            for i in range(1, X)
        ]

    def cz(k):
        return [
            remote(
                c_s[k].at[z_peer(i)], c_z[k].at[i - 1],
                cz_send.at[k, i - 1], cz_recv.at[k, i - 1], at(x, y, z_peer(i), core),
            )
            for i in range(1, Z)
        ]

    def caz(k):
        return [
            remote(
                c_all[k].at[piece], c_all[k].at[piece],
                caz_send.at[k, i - 1], caz_recv.at[k, i - 1], at(x, y, z_peer(i), core),
            )
            for i in range(1, Z)
        ]

    def cax(k):
        own = c_all[k].at[pl.ds(x * Z, Z)]
        return [
            remote(own, own, cax_send.at[k, i - 1], cax_recv.at[k, i - 1], at(x_peer(i), y, z, core))
            for i in range(1, X)
        ]

    def ce(k):
        return [remote(c_all[k], c_all[k], ce_send.at[k], ce_recv.at[k], sibling)]

    five, forty = GROUPS // (X * Z), GROUPS // X

    def gs():
        return [remote(g_own, g_sib, gs_send, gs_recv, sibling)]

    def gx():
        return [
            remote(
                g_own.at[pl.ds(x_peer(i) * forty, forty)], g_x.at[i - 1],
                gx_send.at[i - 1], gx_recv.at[i - 1], at(x_peer(i), y, z, core),
            )
            for i in range(1, X)
        ]

    def gz():
        return [
            remote(
                g_s.at[pl.ds(z_peer(i) * five, five)], g_z.at[i - 1],
                gz_send.at[i - 1], gz_recv.at[i - 1], at(x, y, z_peer(i), core),
            )
            for i in range(1, Z)
        ]

    g_piece = g_all.at[pl.ds(piece * five, five)]

    def gy():
        return [
            remote(g_piece, g_piece, gy_send.at[i - 1], gy_recv, at(x, (y + i) % Y, z, core))
            for i in range(1, Y)
        ]

    def gaz():
        return [
            remote(g_piece, g_piece, gaz_send.at[i - 1], gaz_recv.at[i - 1], at(x, y, z_peer(i), core))
            for i in range(1, Z)
        ]

    def gax():
        own = g_all.at[pl.ds(x * forty, forty)]
        return [
            remote(own, own, gax_send.at[i - 1], gax_recv.at[i - 1], at(x_peer(i), y, z, core))
            for i in range(1, X)
        ]

    def ge(k):
        rows = inv.at[pl.ds(NB * k, NB)]
        return [remote(rows, rows, ge_send.at[k], ge_recv.at[k], sibling)]

    def start(copies):
        for copy in copies:
            copy.start()

    def arrive(copies):
        for copy in copies:
            copy.wait_recv()

    def sent(copies):
        for copy in copies:
            copy.wait_send()

    def panel(start, width):
        rows = slice(start, start + width)
        return split(jnp.concatenate([p[0, rows, :], p[1, rows, :]], axis=1))

    a_load = pltpu.make_async_copy(a_hbm, a, load_sem)
    a_load.start()
    a_load.wait()

    @pl.when(y == 0)
    def _():
        for k in range(4):
            for way in range(2):
                cols = slice(NB * k, NB * k + NB)
                p[way, cols, :] = a[512 * way : 512 * way + 512, cols].T

    pl.semaphore_wait(barrier, len(friends))

    @pl.when(y == 0)
    def _():
        for s in range(SUBS):
            up(s).start()
            down(s).start()
        flipped = [panel(NB * k, NB) for k in range(4)]
        for b, (i, j) in enumerate(BLOCKS):
            block = dot3(flipped[i], flipped[j], ((1,), (1,)))
            for r in range(16):
                g_own[16 * b + r] = block[8 * r : 8 * r + 8, :]

        @pl.when(core == 0)
        def _():
            start(gs())

        @pl.when(core == 1)
        def _():
            arrive(gs())
            g_own[...] = g_own[...] + g_sib[...]
            start(gx())

    for r in range(0, 1024, 256):
        high, low = split(a[r : r + 256, :])
        a_hi[r : r + 256, :] = high
        a_lo[r : r + 256, :] = low

    def p_step(t):
        @pl.when(y == 1)
        def _():
            if t < SUBS:
                up(t).wait_recv()
                up(t).start()
            if 0 <= t - END < SUBS:
                down(t - END).wait_recv()

        @pl.when(y == 2)
        def _():
            if 0 <= t - MID < SUBS:
                up(t - MID).wait_recv()
                up(t - MID).start()
                down(t - MID).wait_recv()
                down(t - MID).start()

        @pl.when(y == 3)
        def _():
            if t < SUBS:
                down(t).wait_recv()
                down(t).start()
            if 0 <= t - END < SUBS:
                up(t - END).wait_recv()

    def compute(k):
        width, lanes = WIDTHS[k], 4 * WIDTHS[k]
        left = panel(STARTS[k], width)
        for tile in range(4):
            cols = slice(256 * tile, 256 * tile + 256)
            part = dot3(left, (a_hi[:, cols], a_lo[:, cols]), ((1,), (0,)))
            size = min(256, lanes)
            for first in range(256 * tile, 256 * tile + 256, size):
                inner = slice(first % lanes, first % lanes + size)
                offset = first - 256 * tile
                for r in range(width // 8):
                    c_own[k][r * (1024 // lanes) + first // lanes, :, inner] = part[
                        8 * r : 8 * r + 8, offset : offset + size
                    ]

    def unfold(k):
        lanes = 4 * WIDTHS[k]
        parts = 1024 // lanes
        for i in range(X * Z):
            rows = STARTS[k] + 8 * (i // parts)
            first = lanes * (i % parts)
            c_full[rows : rows + 8, first : first + lanes] = c_all[k][i]

    def c_stage(k, stage):
        if stage == 1:
            arrive(cs(k))
            c_own[k][...] = c_own[k][...] + c_sib[k][...]
            start(cx(k))
        elif stage == 2:
            arrive(cx(k))
            c_s[k][...] = c_own[k][pl.ds(x * Z, Z)] + c_x[k][0] + (c_x[k][1] + c_x[k][2])
            start(cz(k))
        elif stage == 3:
            arrive(cz(k))
            total = c_s[k][z]
            for i in range(Z - 1):
                total = total + c_z[k][i]
            c_all[k][piece] = total * (1.0 / rows_total)
            start(caz(k))
        elif stage == 4:
            arrive(caz(k))
            start(cax(k))
        elif stage == 5:
            arrive(cax(k))
            start(ce(k))
            unfold(k)

    def bases():
        right = split(inv[...])
        half = N // 2
        for way in range(2):
            rows = slice(512 * way, 512 * way + 512)
            left = split(p[way].T)
            q[rows, :half] = dot3(
                (left[0][:, :half], left[1][:, :half]),
                (right[0][:half, :half], right[1][:half, :half]),
                ((1,), (1,)),
            )
            q[rows, half:] = dot3(left, (right[0][half:], right[1][half:]), ((1,), (1,)))
        q_store.start()

    def coefficients(first, last):
        left = split(inv[first:last, :last])
        for tile in range(4):
            cols = slice(256 * tile, 256 * tile + 256)
            coeff[first:last, cols] = dot3(left, split(c_full[:last, cols]), ((1,), (0,)))

    q_store = pltpu.make_async_copy(q, q_out, store_sem.at[0])
    coeff_store = pltpu.make_async_copy(coeff, coeff_out, store_sem.at[1])

    def g_stage(t):
        if t == READY[0]:

            @pl.when(y == 0)
            def _():
                arrive(gx())
                g_s[...] = g_own[pl.ds(x * forty, forty)] + g_x[0] + (g_x[1] + g_x[2])
                start(gz())

        if t == READY[1]:

            @pl.when(y == 0)
            def _():
                arrive(gz())
                total = g_s[pl.ds(z * five, five)]
                for i in range(Z - 1):
                    total = total + g_z[i]
                g_all[pl.ds(piece * five, five)] = total * (1.0 / rows_total)
                start(gy())

        if t == READY[2] - 1:

            @pl.when(y != 0)
            def _():
                gy()[0].wait_recv()

            start(gaz())
        if t == READY[3]:
            arrive(gaz())
            start(gax())
        if t == READY[4]:
            arrive(gax())
            for b, (i, j) in enumerate(BLOCKS):
                for r in range(16):
                    gram[NB * i + 8 * r : NB * i + 8 * r + 8, NB * j : NB * j + NB] = g_all[16 * b + r]
            factor(gram, inv, lambda k: start(ge(k)))

    due = sorted((READY[k] + 1 + SPACING * (stage - 1), k, stage) for k in range(CHUNKS) for stage in range(1, 6))
    end = SUBS + END
    for t in range(end):
        p_step(t)
        fresh = [k for k in range(CHUNKS) if READY[k] == t]
        for k in fresh:
            compute(k)

        @pl.when(core == 1)
        def _():
            for k in fresh:
                start(cs(k))
            g_stage(t)

        @pl.when(core == 0)
        def _():
            for when, k, stage in due:
                if when == t:
                    c_stage(k, stage)

    early = [k for k in range(CHUNKS) if STARTS[k] + WIDTHS[k] <= N - NB]

    @pl.when(core == 0)
    def _():
        for when, k, stage in due:
            if when >= end and (k, stage) != (CHUNKS - 1, 5):
                c_stage(k, stage)
        for k in range(4):
            arrive(ge(k))
        bases()
        coefficients(0, N - NB)
        c_stage(CHUNKS - 1, 5)
        coefficients(N - NB, N)
        coeff_store.start()

    @pl.when(core == 1)
    def _():
        bases()
        for k in early:
            arrive(ce(k))
            unfold(k)
        coefficients(0, N - NB)
        for k in range(CHUNKS):
            if k not in early:
                arrive(ce(k))
                unfold(k)
        coefficients(N - NB, N)
        coeff_store.start()

    @pl.when((y == 0) | (y == 1) | (y == 2))
    def _():
        for s in range(SUBS):
            up(s).wait_send()

    @pl.when((y == 0) | (y == 2) | (y == 3))
    def _():
        for s in range(SUBS):
            down(s).wait_send()

    @pl.when(core == 0)
    def _():
        @pl.when(y == 0)
        def _():
            sent(gs())

        for k in range(CHUNKS):
            sent(cx(k) + cz(k) + caz(k) + cax(k) + ce(k))

    @pl.when(core == 1)
    def _():
        @pl.when(y == 0)
        def _():
            sent(gx() + gz() + gy())

        for k in range(CHUNKS):
            sent(cs(k))
        for k in range(4):
            sent(ge(k))
        sent(gaz() + gax())

    q_store.wait()
    coeff_store.wait()


def finish_kernel(a, q_in, coeff_in, q, coeff, rest, coeff_hi, coeff_lo):
    @pl.when(pl.program_id(0) == 0)
    def _():
        coeff[...] = coeff_in[...]
        high, low = split(coeff_in[...])
        coeff_hi[...] = high
        coeff_lo[...] = low

    q[...] = q_in[...]
    left = split(q_in[...])
    for tile in range(2):
        lanes = slice(512 * tile, 512 * tile + 512)
        rest[:, lanes] = a[:, lanes] - dot3(left, (coeff_hi[:, lanes], coeff_lo[:, lanes]), ((1,), (0,)))


def vmem(*shape, dtype=F32):
    return pltpu.VMEM(shape, dtype)


def dma(*shape):
    return pltpu.SemaphoreType.DMA(shape) if shape else pltpu.SemaphoreType.DMA


def on_device(matrix):
    rows_total = matrix.shape[0] * lax.axis_size("row")
    any_space = pl.BlockSpec(memory_space=pl.ANY)
    five, forty = GROUPS // (X * Z), GROUPS // X
    pairs = [
        (2, SUBS), (CHUNKS,), (CHUNKS, 3), (CHUNKS, 7), (CHUNKS, 7), (CHUNKS, 3), (CHUNKS,), (), (3,), (7,),
    ]
    sems = [dma(*shape) for shape in pairs for _ in range(2)]
    sizes = [4 * width for width in WIDTHS]
    shapes = ((32, 8), (32, 8), (3, 8, 8), (8, 8), (7, 8), (32, 8))
    basis, coeff = pl.pallas_call(
        functools.partial(gather_kernel, rows_total),
        out_shape=(jax.ShapeDtypeStruct((1024, N), F32), jax.ShapeDtypeStruct((N, 1024), F32)),
        in_specs=[any_space],
        out_specs=[any_space] * 2,
        scratch_shapes=[
            vmem(1024, 1024), vmem(1024, 1024, dtype=BF16), vmem(1024, 1024, dtype=BF16),
            vmem(2, 512, 512), vmem(N, 1024), vmem(1024, N), vmem(N, 1024),
            *[vmem(*shape, size) for shape in shapes for size in sizes],
            vmem(GROUPS, 8, 128), vmem(GROUPS, 8, 128), vmem(3, forty, 8, 128), vmem(forty, 8, 128),
            vmem(7, five, 8, 128), vmem(GROUPS, 8, 128), vmem(N, N), vmem(N, N),
            dma(), dma(2), *sems,
            dma(3), dma(), dma(7), dma(7), dma(3), dma(3), dma(4), dma(4),
        ],
        compiler_params=pltpu.CompilerParams(
            collective_id=0, has_side_effects=True, vmem_limit_bytes=56 * 1024 * 1024
        ),
        name="gather",
    )(matrix)
    tile = 256
    return pl.pallas_call(
        finish_kernel,
        grid=(1024 // tile,),
        out_shape=(
            jax.ShapeDtypeStruct((1024, N), F32),
            jax.ShapeDtypeStruct((N, 1024), F32),
            jax.ShapeDtypeStruct((1024, 1024), F32),
        ),
        in_specs=[
            pl.BlockSpec((tile, 1024), lambda i: (i, 0)),
            pl.BlockSpec((tile, N), lambda i: (i, 0)),
            pl.BlockSpec((N, 1024), lambda i: (0, 0)),
        ],
        out_specs=[
            pl.BlockSpec((tile, N), lambda i: (i, 0)),
            pl.BlockSpec((N, 1024), lambda i: (0, 0)),
            pl.BlockSpec((tile, 1024), lambda i: (i, 0)),
        ],
        scratch_shapes=[vmem(N, 1024, dtype=BF16), vmem(N, 1024, dtype=BF16)],
        compiler_params=pltpu.CompilerParams(vmem_limit_bytes=60 * 1024 * 1024),
        name="finish",
    )(matrix, basis, coeff)


def solution(mesh):
    return jax.shard_map(
        on_device,
        mesh=mesh,
        in_specs=(P("row", "col"),),
        out_specs=(P("row", None), P(None, "col"), P("row", "col")),
        check_vma=False,
    )
```

```python
import functools

import jax
import jax.numpy as jnp
from jax import lax
from jax.experimental import pallas as pl
from jax.experimental.pallas import tpu as pltpu
from jax.sharding import PartitionSpec as P

MESH = pl.DeviceIdType.MESH
F32, BF16 = jnp.float32, jnp.bfloat16
X, Z, Y = 4, 8, 4
N, NB = 512, 128
STEP = 32
SUBS = N // STEP
MID, END = 2, 5
WIDTHS = (128, 128, 128, 64, 64)
CHUNKS = len(WIDTHS)
STARTS = [sum(WIDTHS[:k]) for k in range(CHUNKS)]
READY = [(STARTS[k] + WIDTHS[k]) // STEP - 1 + END for k in range(CHUNKS)]
SHORT = [width == 32 for width in WIDTHS]
STAGES = [4 if short else 5 for short in SHORT]
SPACING = 4
BLOCKS = [(i, j) for j in range(4) for i in range(j, 4)]
GROUPS = 16 * len(BLOCKS)


def split(value):
    high = value.astype(BF16)
    return high, (value - high.astype(F32)).astype(BF16)


def dot3(left, right, dims):
    (left_dim,), (right_dim,) = dims
    left = jnp.concatenate([left[0], left[0], left[1]], axis=left_dim)
    right = jnp.concatenate([right[0], right[1], right[0]], axis=right_dim)
    return lax.dot_general(left, right, (dims, ((), ())), preferred_element_type=F32)


def dot_full(left, right, dims):
    return lax.dot_general(
        left, right, (dims, ((), ())), precision=lax.Precision.HIGHEST, preferred_element_type=F32
    )


def leaf(tiles):
    lane = lax.broadcasted_iota(jnp.int32, (8, 128), 1)
    sub = lax.broadcasted_iota(jnp.int32, (8, 128), 0)
    tiles = list(tiles)
    for r in range(16):
        lo = 8 * r
        group = (lane >= lo) & (lane < lo + 8)
        cols = {
            i: [jnp.broadcast_to(tiles[i][:, lo + m : lo + m + 1], (8, 128)) for m in range(8)]
            for i in range(r, 16)
        }
        pivot = {
            (i, m): jnp.broadcast_to(cols[r][m][i : i + 1, :], (8, 128))
            for m in range(8)
            for i in range(m, 8)
        }
        base = jnp.where(group, (lane - lo == sub).astype(F32), tiles[r])
        rows = [jnp.broadcast_to(base[m : m + 1, :], (8, 128)) for m in range(8)]
        for i in range(r + 1, 16):
            tiles[i] = jnp.where(group, 0.0, tiles[i])
        out = jnp.zeros((8, 128), F32)
        for j in range(8):
            inv = lax.rsqrt(pivot[j, j])
            low = {m: pivot[m, j] * inv for m in range(j + 1, 8)}
            for m in range(j + 1, 8):
                for i in range(m, 8):
                    pivot[i, m] = pivot[i, m] - low[i] * low[m]
            row = rows[j] * inv
            for m in range(j + 1, 8):
                rows[m] = rows[m] - low[m] * row
            out = jnp.where(sub == j, row, out)
            for i in range(r + 1, 16):
                col = cols[i][j] * inv
                for m in range(j + 1, 8):
                    cols[i][m] = cols[i][m] - col * low[m]
                tiles[i] = tiles[i] - col * row
        tiles[r] = jnp.where(lane <= sub + lo, out, 0.0)
    return tiles


def factor(gram, inv, done):
    inv[...] = jnp.zeros_like(inv)
    for k in range(4):
        a, b = k * NB, (k + 1) * NB
        own = jnp.concatenate(leaf([gram[a + 8 * i : a + 8 * i + 8, a:b] for i in range(16)]), axis=0)
        inv[a:b, a:b] = own
        if k:
            inv[a:b, :a] = dot3(split(own), split(inv[a:b, :a]), ((1,), (0,)))
        done(k)
        if k < 3:
            low = dot_full(gram[b:, a:b], own, ((1,), (1,)))
            gram[b:, b:] = gram[b:, b:] - dot_full(low, low, ((1,), (1,)))
            inv[b:, :b] = inv[b:, :b] - dot3(split(low), split(inv[a:b, :b]), ((1,), (0,)))


def gather_kernel(rows_total, a_hbm, q_out, coeff_out, *scratch):
    scratch = list(scratch)

    def take(count):
        taken = scratch[:count]
        del scratch[:count]
        return taken

    a, a_hi, a_lo, p, p_hi, p_lo, c_full, q, coeff = take(9)
    c_own, c_sib, c_x, c_s, c_z, c_all = (take(CHUNKS) for _ in range(6))
    g_own, g_sib, g_x, g_s, g_z, g_all, gram, inv = take(8)
    load_sem, store_sem, p_send, p_recv, cs_send, cs_recv, cx_send, cx_recv, cz_send, cz_recv = take(10)
    caz_send, caz_recv, cax_send, cax_recv, ce_send, ce_recv, gs_send, gs_recv, gx_send, gx_recv = take(10)
    gz_send, gz_recv, gy_send, gy_recv, gaz_send, gaz_recv, gax_send, gax_recv, ge_send, ge_recv = take(10)
    row, y = lax.axis_index("row"), lax.axis_index("col")
    core, z, x = row % 2, (row // 2) % Z, row // (2 * Z)
    piece = x * Z + z

    def at(px, py, pz, pc):
        return ((px * Z + pz) * 2 + pc, py)

    def x_peer(i):
        return (x + i) % X

    def z_peer(i):
        return (z + i) % Z

    def remote(src, dst, send, recv, device):
        return pltpu.make_async_remote_copy(
            src_ref=src, dst_ref=dst, send_sem=send, recv_sem=recv, device_id=device, device_id_type=MESH
        )

    sibling = at(x, y, z, 1 - core)
    barrier = pltpu.get_barrier_semaphore()
    friends = [sibling]
    friends += [at(x_peer(i), y, z, core) for i in range(1, X)]
    friends += [at(x, y, z_peer(i), core) for i in range(1, Z)]
    friends += [at(x, (y + i) % Y, z, core) for i in range(1, Y)]
    for friend in friends:
        pl.semaphore_signal(barrier, inc=1, device_id=friend, device_id_type=MESH)

    def p_copy(way, s, step):
        part = p.at[way, pl.ds(STEP * s, STEP)]
        return remote(part, part, p_send.at[way, s], p_recv.at[way, s], at(x, (y + step) % Y, z, core))

    def up(s):
        return p_copy(0, s, 1)

    def down(s):
        return p_copy(1, s, Y - 1)

    def cs(k):
        return [remote(c_own[k], c_sib[k], cs_send.at[k], cs_recv.at[k], sibling)]

    def cx(k):
        return [
            remote(
                c_own[k].at[pl.ds(x_peer(i) * Z, Z)], c_x[k].at[i - 1],
                cx_send.at[k, i - 1], cx_recv.at[k, i - 1], at(x_peer(i), y, z, core),
            )
            for i in range(1, X)
        ]

    def cz(k):
        if SHORT[k]:
            own = c_z[k].at[z]
            return [
                remote(own, own, cz_send.at[k, i - 1], cz_recv.at[k, i - 1], at(x, y, z_peer(i), core))
                for i in range(1, Z)
            ]
        return [
            remote(
                c_s[k].at[z_peer(i)], c_z[k].at[i - 1],
                cz_send.at[k, i - 1], cz_recv.at[k, i - 1], at(x, y, z_peer(i), core),
            )
            for i in range(1, Z)
        ]

    def caz(k):
        return [
            remote(
                c_all[k].at[piece], c_all[k].at[piece],
                caz_send.at[k, i - 1], caz_recv.at[k, i - 1], at(x, y, z_peer(i), core),
            )
            for i in range(1, Z)
        ]

    def cax(k):
        own = c_all[k].at[pl.ds(x * Z, Z)]
        return [
            remote(own, own, cax_send.at[k, i - 1], cax_recv.at[k, i - 1], at(x_peer(i), y, z, core))
            for i in range(1, X)
        ]

    def ce(k):
        return [remote(c_all[k], c_all[k], ce_send.at[k], ce_recv.at[k], sibling)]

    five, forty = GROUPS // (X * Z), GROUPS // X

    def gs():
        return [remote(g_own, g_sib, gs_send, gs_recv, sibling)]

    def gx():
        return [
            remote(
                g_own.at[pl.ds(x_peer(i) * forty, forty)], g_x.at[i - 1],
                gx_send.at[i - 1], gx_recv.at[i - 1], at(x_peer(i), y, z, core),
            )
            for i in range(1, X)
        ]

    def gz():
        return [
            remote(
                g_s.at[pl.ds(z_peer(i) * five, five)], g_z.at[i - 1],
                gz_send.at[i - 1], gz_recv.at[i - 1], at(x, y, z_peer(i), core),
            )
            for i in range(1, Z)
        ]

    g_piece = g_all.at[pl.ds(piece * five, five)]

    def gy():
        return [
            remote(g_piece, g_piece, gy_send.at[i - 1], gy_recv, at(x, (y + i) % Y, z, core))
            for i in range(1, Y)
        ]

    def gaz():
        return [
            remote(g_piece, g_piece, gaz_send.at[i - 1], gaz_recv.at[i - 1], at(x, y, z_peer(i), core))
            for i in range(1, Z)
        ]

    def gax():
        own = g_all.at[pl.ds(x * forty, forty)]
        return [
            remote(own, own, gax_send.at[i - 1], gax_recv.at[i - 1], at(x_peer(i), y, z, core))
            for i in range(1, X)
        ]

    def ge(k):
        rows = inv.at[pl.ds(NB * k, NB)]
        return [remote(rows, rows, ge_send.at[k], ge_recv.at[k], sibling)]

    def start(copies):
        for copy in copies:
            copy.start()

    def arrive(copies):
        for copy in copies:
            copy.wait_recv()

    def sent(copies):
        for copy in copies:
            copy.wait_send()

    def panel(start, width):
        rows = slice(start, start + width)
        return split(jnp.concatenate([p[0, rows, :], p[1, rows, :]], axis=1))

    def a_load(half):
        cols = pl.ds(512 * half, 512)
        return pltpu.make_async_copy(a_hbm.at[:, cols], a.at[:, cols], load_sem.at[half])

    a_load(0).start()
    a_load(1).start()
    a_load(0).wait()
    pl.semaphore_wait(barrier, len(friends))

    @pl.when(y == 0)
    def _():
        for k in range(4):
            for way in range(2):
                cols = slice(NB * k, NB * k + NB)
                p[way, cols, :] = a[512 * way : 512 * way + 512, cols].T
            for s in range(NB // STEP * k, NB // STEP * (k + 1)):
                up(s).start()
                down(s).start()
        flipped = [panel(NB * k, NB) for k in range(4)]
        for b, (i, j) in enumerate(BLOCKS):
            block = dot3(flipped[i], flipped[j], ((1,), (1,)))
            for r in range(16):
                g_own[16 * b + r] = block[8 * r : 8 * r + 8, :]

        @pl.when(core == 0)
        def _():
            start(gs())

        @pl.when(core == 1)
        def _():
            arrive(gs())
            g_own[...] = g_own[...] + g_sib[...]
            start(gx())

    a_load(1).wait()
    for r in range(0, 1024, 256):
        high, low = split(a[r : r + 256, :])
        a_hi[r : r + 256, :] = high
        a_lo[r : r + 256, :] = low

    def p_step(t):
        @pl.when(y == 1)
        def _():
            if t < SUBS:
                up(t).wait_recv()
                up(t).start()
            if 0 <= t - END < SUBS:
                down(t - END).wait_recv()

        @pl.when(y == 2)
        def _():
            if 0 <= t - MID < SUBS:
                up(t - MID).wait_recv()
                up(t - MID).start()
                down(t - MID).wait_recv()
                down(t - MID).start()

        @pl.when(y == 3)
        def _():
            if t < SUBS:
                down(t).wait_recv()
                down(t).start()
            if 0 <= t - END < SUBS:
                up(t - END).wait_recv()

    def compute(k):
        width, lanes = WIDTHS[k], 4 * WIDTHS[k]
        left = panel(STARTS[k], width)
        for tile in range(4):
            cols = slice(256 * tile, 256 * tile + 256)
            part = dot3(left, (a_hi[:, cols], a_lo[:, cols]), ((1,), (0,)))
            size = min(256, lanes)
            for first in range(256 * tile, 256 * tile + 256, size):
                inner = slice(first % lanes, first % lanes + size)
                offset = first - 256 * tile
                for r in range(width // 8):
                    c_own[k][r * (1024 // lanes) + first // lanes, :, inner] = part[
                        8 * r : 8 * r + 8, offset : offset + size
                    ]

    def turn(start):
        for way in range(2):
            rows, cols = slice(512 * way, 512 * way + 512), slice(start, start + NB)
            high, low = split(p[way, cols, :].T)
            p_hi[rows, cols] = high
            p_lo[rows, cols] = low

    def unfold(k):
        lanes = 4 * WIDTHS[k]
        parts = 1024 // lanes
        for i in range(X * Z):
            rows = STARTS[k] + 8 * (i // parts)
            first = lanes * (i % parts)
            c_full[rows : rows + 8, first : first + lanes] = c_all[k][i]

    def c_stage(k, stage):
        if stage == 1:
            arrive(cs(k))
            c_own[k][...] = c_own[k][...] + c_sib[k][...]
            start(cx(k))
        elif stage == 2:
            arrive(cx(k))
            part = c_s[k] if not SHORT[k] else c_z[k].at[z]
            part[...] = c_own[k][pl.ds(x * Z, Z)] + c_x[k][0] + (c_x[k][1] + c_x[k][2])
            start(cz(k))
        elif stage == 3 and SHORT[k]:
            arrive(cz(k))
            total = c_z[k][0]
            for i in range(1, Z):
                total = total + c_z[k][i]
            c_all[k][pl.ds(x * Z, Z)] = total * (1.0 / rows_total)
            start(cax(k))
        elif stage == 3:
            arrive(cz(k))
            total = c_s[k][z]
            for i in range(Z - 1):
                total = total + c_z[k][i]
            c_all[k][piece] = total * (1.0 / rows_total)
            start(caz(k))
        elif stage == 4 and not SHORT[k]:
            arrive(caz(k))
            start(cax(k))
        else:
            arrive(cax(k))
            start(ce(k))
            unfold(k)

    def bases():
        right = split(inv[...])
        half = N // 2
        for way in range(2):
            rows = slice(512 * way, 512 * way + 512)
            left = p_hi[rows, :], p_lo[rows, :]
            q[rows, :half] = dot3(
                (left[0][:, :half], left[1][:, :half]),
                (right[0][:half, :half], right[1][:half, :half]),
                ((1,), (1,)),
            )
            q[rows, half:] = dot3(left, (right[0][half:], right[1][half:]), ((1,), (1,)))
        q_store.start()

    def coefficients(first, last):
        left = split(inv[first:last, :last])
        for tile in range(4):
            cols = slice(256 * tile, 256 * tile + 256)
            coeff[first:last, cols] = dot3(left, split(c_full[:last, cols]), ((1,), (0,)))

    q_store = pltpu.make_async_copy(q, q_out, store_sem.at[0])

    def coeff_store(late):
        rows = pl.ds((N - NB) * late, NB if late else N - NB)
        return pltpu.make_async_copy(coeff.at[rows], coeff_out.at[rows], store_sem.at[1 + late])

    def g_stage(t):
        if t == READY[0]:

            @pl.when(y == 0)
            def _():
                arrive(gx())
                g_s[...] = g_own[pl.ds(x * forty, forty)] + g_x[0] + (g_x[1] + g_x[2])
                start(gz())

        if t == READY[1]:

            @pl.when(y == 0)
            def _():
                arrive(gz())
                total = g_s[pl.ds(z * five, five)]
                for i in range(Z - 1):
                    total = total + g_z[i]
                g_all[pl.ds(piece * five, five)] = total * (1.0 / rows_total)
                start(gy())

        if t == READY[2] - 1:

            @pl.when(y != 0)
            def _():
                gy()[0].wait_recv()

            start(gaz())
        if t == READY[3]:
            arrive(gaz())
            start(gax())
        if t == READY[-1]:
            arrive(gax())
            for b, (i, j) in enumerate(BLOCKS):
                for r in range(16):
                    gram[NB * i + 8 * r : NB * i + 8 * r + 8, NB * j : NB * j + NB] = g_all[16 * b + r]
            factor(gram, inv, lambda k: start(ge(k)))

    due = sorted((READY[k] + 1 + SPACING * (stage - 1), k, stage) for k in range(CHUNKS) for stage in range(1, STAGES[k] + 1))
    end = SUBS + END
    for t in range(end):
        p_step(t)
        fresh = [k for k in range(CHUNKS) if READY[k] == t]
        for k in fresh:
            compute(k)

        @pl.when(core == 1)
        def _():
            for k in fresh:
                start(cs(k))
                if (STARTS[k] + WIDTHS[k]) % NB == 0:
                    turn(STARTS[k] + WIDTHS[k] - NB)
            g_stage(t)

        @pl.when(core == 0)
        def _():
            for when, k, stage in due:
                if when == t:
                    c_stage(k, stage)
            for k in fresh:
                if (STARTS[k] + WIDTHS[k]) % NB == 0:
                    turn(STARTS[k] + WIDTHS[k] - NB)

    early = [k for k in range(CHUNKS) if STARTS[k] + WIDTHS[k] <= N - NB]

    @pl.when(core == 0)
    def _():
        for when, k, stage in due:
            if when >= end:
                c_stage(k, stage)
        for k in range(4):
            arrive(ge(k))
        bases()
        coefficients(0, N - NB)
        coeff_store(0).start()
        coefficients(N - NB, N)
        coeff_store(1).start()

    @pl.when(core == 1)
    def _():
        bases()
        for k in early:
            arrive(ce(k))
            unfold(k)
        coefficients(0, N - NB)
        coeff_store(0).start()
        for k in range(CHUNKS):
            if k not in early:
                arrive(ce(k))
                unfold(k)
        coefficients(N - NB, N)
        coeff_store(1).start()

    @pl.when((y == 0) | (y == 1) | (y == 2))
    def _():
        for s in range(SUBS):
            up(s).wait_send()

    @pl.when((y == 0) | (y == 2) | (y == 3))
    def _():
        for s in range(SUBS):
            down(s).wait_send()

    @pl.when(core == 0)
    def _():
        @pl.when(y == 0)
        def _():
            sent(gs())

        for k in range(CHUNKS):
            sent(cx(k) + cz(k) + ([] if SHORT[k] else caz(k)) + cax(k) + ce(k))

    @pl.when(core == 1)
    def _():
        @pl.when(y == 0)
        def _():
            sent(gx() + gz() + gy())

        for k in range(CHUNKS):
            sent(cs(k))
        for k in range(4):
            sent(ge(k))
        sent(gaz() + gax())

    q_store.wait()
    coeff_store(0).wait()
    coeff_store(1).wait()


def finish_kernel(a, q_in, coeff_in, q, coeff, rest, coeff_hi, coeff_lo):
    @pl.when(pl.program_id(0) == 0)
    def _():
        coeff[...] = coeff_in[...]
        high, low = split(coeff_in[...])
        coeff_hi[...] = high
        coeff_lo[...] = low

    q[...] = q_in[...]
    left = split(q_in[...])
    for tile in range(2):
        lanes = slice(512 * tile, 512 * tile + 512)
        rest[:, lanes] = a[:, lanes] - dot3(left, (coeff_hi[:, lanes], coeff_lo[:, lanes]), ((1,), (0,)))


def vmem(*shape, dtype=F32):
    return pltpu.VMEM(shape, dtype)


def dma(*shape):
    return pltpu.SemaphoreType.DMA(shape) if shape else pltpu.SemaphoreType.DMA


def on_device(matrix):
    rows_total = matrix.shape[0] * lax.axis_size("row")
    any_space = pl.BlockSpec(memory_space=pl.ANY)
    five, forty = GROUPS // (X * Z), GROUPS // X
    pairs = [
        (2, SUBS), (CHUNKS,), (CHUNKS, 3), (CHUNKS, 7), (CHUNKS, 7), (CHUNKS, 3), (CHUNKS,), (), (3,), (7,),
    ]
    sems = [dma(*shape) for shape in pairs for _ in range(2)]
    sizes = [4 * width for width in WIDTHS]
    shapes = ((32, 8), (32, 8), (3, 8, 8), (8, 8), (7, 8), (32, 8))
    short_shapes = (*shapes[:4], (8, 8, 8), shapes[5])
    sums = [
        vmem(*(short_shape if short else shape), size)
        for shape, short_shape in zip(shapes, short_shapes)
        for size, short in zip(sizes, SHORT)
    ]
    basis, coeff = pl.pallas_call(
        functools.partial(gather_kernel, rows_total),
        out_shape=(jax.ShapeDtypeStruct((1024, N), F32), jax.ShapeDtypeStruct((N, 1024), F32)),
        in_specs=[any_space],
        out_specs=[any_space] * 2,
        scratch_shapes=[
            vmem(1024, 1024), vmem(1024, 1024, dtype=BF16), vmem(1024, 1024, dtype=BF16),
            vmem(2, 512, 512), vmem(1024, N, dtype=BF16), vmem(1024, N, dtype=BF16), vmem(N, 1024), vmem(1024, N), vmem(N, 1024),
            *sums,
            vmem(GROUPS, 8, 128), vmem(GROUPS, 8, 128), vmem(3, forty, 8, 128), vmem(forty, 8, 128),
            vmem(7, five, 8, 128), vmem(GROUPS, 8, 128), vmem(N, N), vmem(N, N),
            dma(2), dma(3), *sems,
            dma(3), dma(), dma(7), dma(7), dma(3), dma(3), dma(4), dma(4),
        ],
        compiler_params=pltpu.CompilerParams(
            collective_id=0, has_side_effects=True, vmem_limit_bytes=56 * 1024 * 1024
        ),
        name="gather",
    )(matrix)
    tile = 256
    return pl.pallas_call(
        finish_kernel,
        grid=(1024 // tile,),
        out_shape=(
            jax.ShapeDtypeStruct((1024, N), F32),
            jax.ShapeDtypeStruct((N, 1024), F32),
            jax.ShapeDtypeStruct((1024, 1024), F32),
        ),
        in_specs=[
            pl.BlockSpec((tile, 1024), lambda i: (i, 0)),
            pl.BlockSpec((tile, N), lambda i: (i, 0)),
            pl.BlockSpec((N, 1024), lambda i: (0, 0)),
        ],
        out_specs=[
            pl.BlockSpec((tile, N), lambda i: (i, 0)),
            pl.BlockSpec((N, 1024), lambda i: (0, 0)),
            pl.BlockSpec((tile, 1024), lambda i: (i, 0)),
        ],
        scratch_shapes=[vmem(N, 1024, dtype=BF16), vmem(N, 1024, dtype=BF16)],
        compiler_params=pltpu.CompilerParams(vmem_limit_bytes=60 * 1024 * 1024),
        name="finish",
    )(matrix, basis, coeff)


def solution(mesh):
    return jax.shard_map(
        on_device,
        mesh=mesh,
        in_specs=(P("row", "col"),),
        out_specs=(P("row", None), P(None, "col"), P("row", "col")),
        check_vma=False,
    )
```

```python
import functools

import jax
import jax.numpy as jnp
from jax import lax
from jax.experimental import pallas as pl
from jax.experimental.pallas import tpu as pltpu
from jax.sharding import PartitionSpec as P

MESH = pl.DeviceIdType.MESH
F32, BF16 = jnp.float32, jnp.bfloat16
X, Z, Y = 4, 8, 4
N, NB = 512, 128
STEP = 32
SUBS = N // STEP
MID, END = 2, 5
WIDTHS = (128, 128, 128, 64, 64)
CHUNKS = len(WIDTHS)
STARTS = [sum(WIDTHS[:k]) for k in range(CHUNKS)]
READY = [(STARTS[k] + WIDTHS[k]) // STEP - 1 + END for k in range(CHUNKS)]
SHORT = [width == 32 for width in WIDTHS]
STAGES = [4 if short else 5 for short in SHORT]
SPACING = 4
BLOCKS = [(i, j) for j in range(4) for i in range(j, 4)]
GROUPS = 16 * len(BLOCKS)


def split(value):
    high = value.astype(BF16)
    return high, (value - high.astype(F32)).astype(BF16)


def dot3(left, right, dims):
    (left_dim,), (right_dim,) = dims
    left = jnp.concatenate([left[0], left[0], left[1]], axis=left_dim)
    right = jnp.concatenate([right[0], right[1], right[0]], axis=right_dim)
    return lax.dot_general(left, right, (dims, ((), ())), preferred_element_type=F32)


def dot_full(left, right, dims):
    return lax.dot_general(
        left, right, (dims, ((), ())), precision=lax.Precision.HIGHEST, preferred_element_type=F32
    )


def leaf(tiles):
    lane = lax.broadcasted_iota(jnp.int32, (8, 128), 1)
    sub = lax.broadcasted_iota(jnp.int32, (8, 128), 0)
    tiles = list(tiles)
    for r in range(16):
        lo = 8 * r
        group = (lane >= lo) & (lane < lo + 8)
        cols = {
            i: [jnp.broadcast_to(tiles[i][:, lo + m : lo + m + 1], (8, 128)) for m in range(8)]
            for i in range(r, 16)
        }
        pivot = {
            (i, m): jnp.broadcast_to(cols[r][m][i : i + 1, :], (8, 128))
            for m in range(8)
            for i in range(m, 8)
        }
        base = jnp.where(group, (lane - lo == sub).astype(F32), tiles[r])
        rows = [jnp.broadcast_to(base[m : m + 1, :], (8, 128)) for m in range(8)]
        for i in range(r + 1, 16):
            tiles[i] = jnp.where(group, 0.0, tiles[i])
        out = jnp.zeros((8, 128), F32)
        for j in range(8):
            inv = lax.rsqrt(pivot[j, j])
            low = {m: pivot[m, j] * inv for m in range(j + 1, 8)}
            for m in range(j + 1, 8):
                for i in range(m, 8):
                    pivot[i, m] = pivot[i, m] - low[i] * low[m]
            row = rows[j] * inv
            for m in range(j + 1, 8):
                rows[m] = rows[m] - low[m] * row
            out = jnp.where(sub == j, row, out)
            for i in range(r + 1, 16):
                col = cols[i][j] * inv
                for m in range(j + 1, 8):
                    cols[i][m] = cols[i][m] - col * low[m]
                tiles[i] = tiles[i] - col * row
        tiles[r] = jnp.where(lane <= sub + lo, out, 0.0)
    return tiles


def factor(gram, inv, done):
    inv[...] = jnp.zeros_like(inv)
    for k in range(4):
        a, b = k * NB, (k + 1) * NB
        own = jnp.concatenate(leaf([gram[a + 8 * i : a + 8 * i + 8, a:b] for i in range(16)]), axis=0)
        inv[a:b, a:b] = own
        if k:
            inv[a:b, :a] = dot3(split(own), split(inv[a:b, :a]), ((1,), (0,)))
        done(k)
        if k < 3:
            low = dot_full(gram[b:, a:b], own, ((1,), (1,)))
            gram[b:, b:] = gram[b:, b:] - dot_full(low, low, ((1,), (1,)))
            inv[b:, :b] = inv[b:, :b] - dot3(split(low), split(inv[a:b, :b]), ((1,), (0,)))


def gather_kernel(rows_total, a_hbm, q_out, coeff_out, *scratch):
    scratch = list(scratch)

    def take(count):
        taken = scratch[:count]
        del scratch[:count]
        return taken

    a, a_hi, a_lo, p, p_hi, p_lo, c_full, q, coeff = take(9)
    c_own, c_sib, c_x, c_s, c_z, c_all = (take(CHUNKS) for _ in range(6))
    g_own, g_sib, g_x, g_s, g_z, g_all, gram, inv = take(8)
    load_sem, store_sem, p_send, p_recv, cs_send, cs_recv, cx_send, cx_recv, cz_send, cz_recv = take(10)
    caz_send, caz_recv, cax_send, cax_recv, ce_send, ce_recv, gs_send, gs_recv, gx_send, gx_recv = take(10)
    gz_send, gz_recv, gy_send, gy_recv, gaz_send, gaz_recv, gax_send, gax_recv, ge_send, ge_recv = take(10)
    row, y = lax.axis_index("row"), lax.axis_index("col")
    core, z, x = row % 2, (row // 2) % Z, row // (2 * Z)
    piece = x * Z + z

    def at(px, py, pz, pc):
        return ((px * Z + pz) * 2 + pc, py)

    def x_peer(i):
        return (x + i) % X

    def z_peer(i):
        return (z + i) % Z

    def remote(src, dst, send, recv, device):
        return pltpu.make_async_remote_copy(
            src_ref=src, dst_ref=dst, send_sem=send, recv_sem=recv, device_id=device, device_id_type=MESH
        )

    sibling = at(x, y, z, 1 - core)
    barrier = pltpu.get_barrier_semaphore()
    friends = [sibling]
    friends += [at(x_peer(i), y, z, core) for i in range(1, X)]
    friends += [at(x, y, z_peer(i), core) for i in range(1, Z)]
    friends += [at(x, (y + i) % Y, z, core) for i in range(1, Y)]
    for friend in friends:
        pl.semaphore_signal(barrier, inc=1, device_id=friend, device_id_type=MESH)

    def p_copy(way, s, step):
        part = p.at[way, pl.ds(STEP * s, STEP)]
        return remote(part, part, p_send.at[way, s], p_recv.at[way, s], at(x, (y + step) % Y, z, core))

    def up(s):
        return p_copy(0, s, 1)

    def down(s):
        return p_copy(1, s, Y - 1)

    def cs(k):
        return [remote(c_own[k], c_sib[k], cs_send.at[k], cs_recv.at[k], sibling)]

    def cx(k):
        return [
            remote(
                c_own[k].at[pl.ds(x_peer(i) * Z, Z)], c_x[k].at[i - 1],
                cx_send.at[k, i - 1], cx_recv.at[k, i - 1], at(x_peer(i), y, z, core),
            )
            for i in range(1, X)
        ]

    def cz(k):
        if SHORT[k]:
            own = c_z[k].at[z]
            return [
                remote(own, own, cz_send.at[k, i - 1], cz_recv.at[k, i - 1], at(x, y, z_peer(i), core))
                for i in range(1, Z)
            ]
        return [
            remote(
                c_s[k].at[z_peer(i)], c_z[k].at[i - 1],
                cz_send.at[k, i - 1], cz_recv.at[k, i - 1], at(x, y, z_peer(i), core),
            )
            for i in range(1, Z)
        ]

    def caz(k):
        return [
            remote(
                c_all[k].at[piece], c_all[k].at[piece],
                caz_send.at[k, i - 1], caz_recv.at[k, i - 1], at(x, y, z_peer(i), core),
            )
            for i in range(1, Z)
        ]

    def cax(k):
        own = c_all[k].at[pl.ds(x * Z, Z)]
        return [
            remote(own, own, cax_send.at[k, i - 1], cax_recv.at[k, i - 1], at(x_peer(i), y, z, core))
            for i in range(1, X)
        ]

    def ce(k):
        return [remote(c_all[k], c_all[k], ce_send.at[k], ce_recv.at[k], sibling)]

    five, forty = GROUPS // (X * Z), GROUPS // X

    def gs():
        return [remote(g_own, g_sib, gs_send, gs_recv, sibling)]

    def gx():
        return [
            remote(
                g_own.at[pl.ds(x_peer(i) * forty, forty)], g_x.at[i - 1],
                gx_send.at[i - 1], gx_recv.at[i - 1], at(x_peer(i), y, z, core),
            )
            for i in range(1, X)
        ]

    def gz():
        return [
            remote(
                g_s.at[pl.ds(z_peer(i) * five, five)], g_z.at[i - 1],
                gz_send.at[i - 1], gz_recv.at[i - 1], at(x, y, z_peer(i), core),
            )
            for i in range(1, Z)
        ]

    g_piece = g_all.at[pl.ds(piece * five, five)]

    def gy():
        return [
            remote(g_piece, g_piece, gy_send.at[i - 1], gy_recv, at(x, (y + i) % Y, z, core))
            for i in range(1, Y)
        ]

    def gaz():
        return [
            remote(g_piece, g_piece, gaz_send.at[i - 1], gaz_recv.at[i - 1], at(x, y, z_peer(i), core))
            for i in range(1, Z)
        ]

    def gax():
        own = g_all.at[pl.ds(x * forty, forty)]
        return [
            remote(own, own, gax_send.at[i - 1], gax_recv.at[i - 1], at(x_peer(i), y, z, core))
            for i in range(1, X)
        ]

    def ge(k):
        rows = inv.at[pl.ds(NB * k, NB)]
        return [remote(rows, rows, ge_send.at[k], ge_recv.at[k], sibling)]

    def start(copies):
        for copy in copies:
            copy.start()

    def arrive(copies):
        for copy in copies:
            copy.wait_recv()

    def sent(copies):
        for copy in copies:
            copy.wait_send()

    def panel(start, width):
        rows = slice(start, start + width)
        return split(jnp.concatenate([p[0, rows, :], p[1, rows, :]], axis=1))

    def a_load(half):
        cols = pl.ds(512 * half, 512)
        return pltpu.make_async_copy(a_hbm.at[:, cols], a.at[:, cols], load_sem.at[half])

    a_load(0).start()
    a_load(1).start()
    a_load(0).wait()
    pl.semaphore_wait(barrier, len(friends))

    @pl.when(y == 0)
    def _():
        for k in range(4):
            for way in range(2):
                cols = slice(NB * k, NB * k + NB)
                p[way, cols, :] = a[512 * way : 512 * way + 512, cols].T
            for s in range(NB // STEP * k, NB // STEP * (k + 1)):
                up(s).start()
                down(s).start()
        flipped = [panel(NB * k, NB) for k in range(4)]
        for b, (i, j) in enumerate(BLOCKS):
            block = dot3(flipped[i], flipped[j], ((1,), (1,)))
            for r in range(16):
                g_own[16 * b + r] = block[8 * r : 8 * r + 8, :]

        @pl.when(core == 0)
        def _():
            start(gs())

        @pl.when(core == 1)
        def _():
            arrive(gs())
            g_own[...] = g_own[...] + g_sib[...]
            start(gx())

    a_load(1).wait()
    for r in range(0, 1024, 256):
        high, low = split(a[r : r + 256, :])
        a_hi[r : r + 256, :] = high
        a_lo[r : r + 256, :] = low

    def p_step(t):
        @pl.when(y == 1)
        def _():
            if t < SUBS:
                up(t).wait_recv()
                up(t).start()
            if 0 <= t - END < SUBS:
                down(t - END).wait_recv()

        @pl.when(y == 2)
        def _():
            if 0 <= t - MID < SUBS:
                up(t - MID).wait_recv()
                up(t - MID).start()
                down(t - MID).wait_recv()
                down(t - MID).start()

        @pl.when(y == 3)
        def _():
            if t < SUBS:
                down(t).wait_recv()
                down(t).start()
            if 0 <= t - END < SUBS:
                up(t - END).wait_recv()

    def compute(k):
        width, lanes = WIDTHS[k], 4 * WIDTHS[k]
        left = panel(STARTS[k], width)
        for tile in range(4):
            cols = slice(256 * tile, 256 * tile + 256)
            part = dot3(left, (a_hi[:, cols], a_lo[:, cols]), ((1,), (0,)))
            size = min(256, lanes)
            for first in range(256 * tile, 256 * tile + 256, size):
                inner = slice(first % lanes, first % lanes + size)
                offset = first - 256 * tile
                for r in range(width // 8):
                    c_own[k][r * (1024 // lanes) + first // lanes, :, inner] = part[
                        8 * r : 8 * r + 8, offset : offset + size
                    ]

    def turn(start):
        for way in range(2):
            rows, cols = slice(512 * way, 512 * way + 512), slice(start, start + NB)
            high, low = split(p[way, cols, :].T)
            p_hi[rows, cols] = high
            p_lo[rows, cols] = low

    def unfold(k):
        lanes = 4 * WIDTHS[k]
        parts = 1024 // lanes
        for i in range(X * Z):
            rows = STARTS[k] + 8 * (i // parts)
            first = lanes * (i % parts)
            c_full[rows : rows + 8, first : first + lanes] = c_all[k][i]

    def c_stage(k, stage):
        if stage == 1:
            arrive(cs(k))
            c_own[k][...] = c_own[k][...] + c_sib[k][...]
            start(cx(k))
        elif stage == 2:
            arrive(cx(k))
            part = c_s[k] if not SHORT[k] else c_z[k].at[z]
            part[...] = c_own[k][pl.ds(x * Z, Z)] + c_x[k][0] + (c_x[k][1] + c_x[k][2])
            start(cz(k))
        elif stage == 3 and SHORT[k]:
            arrive(cz(k))
            total = c_z[k][0]
            for i in range(1, Z):
                total = total + c_z[k][i]
            c_all[k][pl.ds(x * Z, Z)] = total * (1.0 / rows_total)
            start(cax(k))
        elif stage == 3:
            arrive(cz(k))
            total = c_s[k][z]
            for i in range(Z - 1):
                total = total + c_z[k][i]
            c_all[k][piece] = total * (1.0 / rows_total)
            start(caz(k))
        elif stage == 4 and not SHORT[k]:
            arrive(caz(k))
            start(cax(k))
        else:
            arrive(cax(k))
            start(ce(k))
            unfold(k)

    def bases():
        right = split(inv[...])
        half = N // 2
        for way in range(2):
            rows = slice(512 * way, 512 * way + 512)
            left = p_hi[rows, :], p_lo[rows, :]
            q[rows, :half] = dot3(
                (left[0][:, :half], left[1][:, :half]),
                (right[0][:half, :half], right[1][:half, :half]),
                ((1,), (1,)),
            )
            q[rows, half:] = dot3(left, (right[0][half:], right[1][half:]), ((1,), (1,)))
        q_store.start()

    def coefficients(first, last):
        left = split(inv[first:last, :last])
        for tile in range(4):
            cols = slice(256 * tile, 256 * tile + 256)
            coeff[first:last, cols] = dot3(left, split(c_full[:last, cols]), ((1,), (0,)))

    q_store = pltpu.make_async_copy(q, q_out, store_sem.at[0])

    def coeff_store(late):
        rows = pl.ds((N - NB) * late, NB if late else N - NB)
        return pltpu.make_async_copy(coeff.at[rows], coeff_out.at[rows], store_sem.at[1 + late])

    def g_stage(t):
        if t == READY[0]:

            @pl.when(y == 0)
            def _():
                arrive(gx())
                g_s[...] = g_own[pl.ds(x * forty, forty)] + g_x[0] + (g_x[1] + g_x[2])
                start(gz())

        if t == READY[1]:

            @pl.when(y == 0)
            def _():
                arrive(gz())
                total = g_s[pl.ds(z * five, five)]
                for i in range(Z - 1):
                    total = total + g_z[i]
                g_all[pl.ds(piece * five, five)] = total * (1.0 / rows_total)
                start(gy())

        if t == READY[2] - 1:

            @pl.when(y != 0)
            def _():
                gy()[0].wait_recv()

            start(gaz())
        if t == READY[3]:
            arrive(gaz())
            start(gax())
        if t == READY[-1]:
            arrive(gax())
            for b, (i, j) in enumerate(BLOCKS):
                for r in range(16):
                    gram[NB * i + 8 * r : NB * i + 8 * r + 8, NB * j : NB * j + NB] = g_all[16 * b + r]
            factor(gram, inv, lambda k: start(ge(k)))

    due = sorted((READY[k] + 1 + SPACING * (stage - 1), k, stage) for k in range(CHUNKS) for stage in range(1, STAGES[k] + 1))
    end = SUBS + END
    for t in range(end):
        p_step(t)
        fresh = [k for k in range(CHUNKS) if READY[k] == t]
        for k in fresh:
            compute(k)

        @pl.when(core == 1)
        def _():
            for k in fresh:
                start(cs(k))
                if (STARTS[k] + WIDTHS[k]) % NB == 0:
                    turn(STARTS[k] + WIDTHS[k] - NB)
            g_stage(t)

        @pl.when(core == 0)
        def _():
            for when, k, stage in due:
                if when == t:
                    c_stage(k, stage)
            for k in fresh:
                if (STARTS[k] + WIDTHS[k]) % NB == 0:
                    turn(STARTS[k] + WIDTHS[k] - NB)

    early = [k for k in range(CHUNKS) if STARTS[k] + WIDTHS[k] <= N - NB]

    @pl.when(core == 0)
    def _():
        for when, k, stage in due:
            if when >= end:
                c_stage(k, stage)
        for k in range(4):
            arrive(ge(k))
        bases()
        coefficients(0, N - NB)
        coeff_store(0).start()
        coefficients(N - NB, N)
        coeff_store(1).start()

    @pl.when(core == 1)
    def _():
        bases()
        for k in early:
            arrive(ce(k))
            unfold(k)
        coefficients(0, N - NB)
        coeff_store(0).start()
        for k in range(CHUNKS):
            if k not in early:
                arrive(ce(k))
                unfold(k)
        coefficients(N - NB, N)
        coeff_store(1).start()

    @pl.when((y == 0) | (y == 1) | (y == 2))
    def _():
        for s in range(SUBS):
            up(s).wait_send()

    @pl.when((y == 0) | (y == 2) | (y == 3))
    def _():
        for s in range(SUBS):
            down(s).wait_send()

    @pl.when(core == 0)
    def _():
        @pl.when(y == 0)
        def _():
            sent(gs())

        for k in range(CHUNKS):
            sent(cx(k) + cz(k) + ([] if SHORT[k] else caz(k)) + cax(k) + ce(k))

    @pl.when(core == 1)
    def _():
        @pl.when(y == 0)
        def _():
            sent(gx() + gz() + gy())

        for k in range(CHUNKS):
            sent(cs(k))
        for k in range(4):
            sent(ge(k))
        sent(gaz() + gax())

    q_store.wait()
    coeff_store(0).wait()
    coeff_store(1).wait()


def finish_kernel(a, q_in, coeff_in, q, coeff, rest, coeff_hi, coeff_lo):
    @pl.when(pl.program_id(0) == 0)
    def _():
        coeff[...] = coeff_in[...]
        high, low = split(coeff_in[...])
        coeff_hi[...] = high
        coeff_lo[...] = low

    q[...] = q_in[...]
    left = split(q_in[...])
    for tile in range(2):
        lanes = slice(512 * tile, 512 * tile + 512)
        rest[:, lanes] = a[:, lanes] - dot3(left, (coeff_hi[:, lanes], coeff_lo[:, lanes]), ((1,), (0,)))


def vmem(*shape, dtype=F32):
    return pltpu.VMEM(shape, dtype)


def dma(*shape):
    return pltpu.SemaphoreType.DMA(shape) if shape else pltpu.SemaphoreType.DMA


def on_device(matrix):
    rows_total = matrix.shape[0] * lax.axis_size("row")
    any_space = pl.BlockSpec(memory_space=pl.ANY)
    five, forty = GROUPS // (X * Z), GROUPS // X
    pairs = [
        (2, SUBS), (CHUNKS,), (CHUNKS, 3), (CHUNKS, 7), (CHUNKS, 7), (CHUNKS, 3), (CHUNKS,), (), (3,), (7,),
    ]
    sems = [dma(*shape) for shape in pairs for _ in range(2)]
    sizes = [4 * width for width in WIDTHS]
    shapes = ((32, 8), (32, 8), (3, 8, 8), (8, 8), (7, 8), (32, 8))
    short_shapes = (*shapes[:4], (8, 8, 8), shapes[5])
    sums = [
        vmem(*(short_shape if short else shape), size)
        for shape, short_shape in zip(shapes, short_shapes)
        for size, short in zip(sizes, SHORT)
    ]
    basis, coeff = pl.pallas_call(
        functools.partial(gather_kernel, rows_total),
        out_shape=(jax.ShapeDtypeStruct((1024, N), F32), jax.ShapeDtypeStruct((N, 1024), F32)),
        in_specs=[any_space],
        out_specs=[any_space] * 2,
        scratch_shapes=[
            vmem(1024, 1024), vmem(1024, 1024, dtype=BF16), vmem(1024, 1024, dtype=BF16),
            vmem(2, 512, 512), vmem(1024, N, dtype=BF16), vmem(1024, N, dtype=BF16), vmem(N, 1024), vmem(1024, N), vmem(N, 1024),
            *sums,
            vmem(GROUPS, 8, 128), vmem(GROUPS, 8, 128), vmem(3, forty, 8, 128), vmem(forty, 8, 128),
            vmem(7, five, 8, 128), vmem(GROUPS, 8, 128), vmem(N, N), vmem(N, N),
            dma(2), dma(3), *sems,
            dma(3), dma(), dma(7), dma(7), dma(3), dma(3), dma(4), dma(4),
        ],
        compiler_params=pltpu.CompilerParams(
            collective_id=0, has_side_effects=True, vmem_limit_bytes=56 * 1024 * 1024
        ),
        name="gather",
    )(matrix)
    tile = 512
    return pl.pallas_call(
        finish_kernel,
        grid=(1024 // tile,),
        out_shape=(
            jax.ShapeDtypeStruct((1024, N), F32),
            jax.ShapeDtypeStruct((N, 1024), F32),
            jax.ShapeDtypeStruct((1024, 1024), F32),
        ),
        in_specs=[
            pl.BlockSpec((tile, 1024), lambda i: (i, 0)),
            pl.BlockSpec((tile, N), lambda i: (i, 0)),
            pl.BlockSpec((N, 1024), lambda i: (0, 0)),
        ],
        out_specs=[
            pl.BlockSpec((tile, N), lambda i: (i, 0)),
            pl.BlockSpec((N, 1024), lambda i: (0, 0)),
            pl.BlockSpec((tile, 1024), lambda i: (i, 0)),
        ],
        scratch_shapes=[vmem(N, 1024, dtype=BF16), vmem(N, 1024, dtype=BF16)],
        compiler_params=pltpu.CompilerParams(vmem_limit_bytes=60 * 1024 * 1024),
        name="finish",
    )(matrix, basis, coeff)


def solution(mesh):
    return jax.shard_map(
        on_device,
        mesh=mesh,
        in_specs=(P("row", "col"),),
        out_specs=(P("row", None), P(None, "col"), P("row", "col")),
        check_vma=False,
    )
```
